32 devices in a mesh: dp: 8 (over z, y), section: 4 (over x, core).
Axes of the slice: x: 2, y: 2, z: 4, core: 2. Of those that a mesh axis runs over, the one named last changes fastest.
Arguments:
- inputs: bfloat16 [8192, 768], P('dp'), may hold values from -6 to 6
- cotangent: bfloat16 [8192, 768], P('dp'), may hold values from -6 to 6
- in_master: float32 [4, 768, 3072], P('section', 'dp'), may hold values from -3 to 3
- in_first: float32 [4, 768, 3072], P('section', 'dp'), may hold values from -60 to 60
- in_second: float32 [4, 768, 3072], P('section', 'dp'), may hold values from 10 to 1000
- down_master: float32 [4, 1536, 768], P('section', 'dp'), may hold values from -0.109375 to 0.109375
- down_first: float32 [4, 1536, 768], P('section', 'dp'), may hold values from -60 to 60
- down_second: float32 [4, 1536, 768], P('section', 'dp'), may hold values from 10 to 1000
- vec_master: float32 [4, 4608], P('section', 'dp'), may hold values from -1 to 2
- vec_first: float32 [4, 4608], P('section', 'dp'), may hold values from -60 to 60
- vec_second: float32 [4, 4608], P('section', 'dp'), may hold values from 10 to 1000
Outputs:
- section_outputs: bfloat16 [4, 8192, 768], P('section', 'dp')
- section_input_grads: bfloat16 [4, 8192, 768], P('section', 'dp')
- in_grad: float32 [4, 768, 3072], P('section', 'dp')
- down_grad: float32 [4, 1536, 768], P('section', 'dp')
- vec_grad: float32 [4, 4608], P('section', 'dp')
- in_step: float32 [4, 768, 3072], P('section', 'dp')
- in_first_new: float32 [4, 768, 3072], P('section', 'dp')
- in_second_new: float32 [4, 768, 3072], P('section', 'dp')
- down_step: float32 [4, 1536, 768], P('section', 'dp')
- down_first_new: float32 [4, 1536, 768], P('section', 'dp')
- down_second_new: float32 [4, 1536, 768], P('section', 'dp')
- vec_step: float32 [4, 4608], P('section', 'dp')
- vec_first_new: float32 [4, 4608], P('section', 'dp')
- vec_second_new: float32 [4, 4608], P('section', 'dp')
The draws below stay inside these ranges and needn't reach their ends.
All inputs are finite; a program needn't handle non-finite values.
Results may differ from the reference program's by a relative error of at most 0.02.
Values may be sent and summed in bfloat16 or wider, within the bound.
No kernel may reach another device: no remote copies, remote signals or barrier semaphores. Data moves between devices by JAX's collectives and lax.ppermute only.
A program may use at most 384 MiB of HBM per device.

```python
import math
import jax
import jax.numpy as jnp
from jax import lax

D = 768
HEADS = 12
HEAD_DIM = 64
FF = 3072
LAYERS = 2
SEQ = 512
SECTIONS = 4
VEC = 4608
TOKENS = 8192


def draw_in_master(key, part):
    key = jax.random.fold_in(key, 11)
    base = jnp.clip(jax.random.normal(key, (SECTIONS, D, FF), jnp.float32), -4.0, 4.0)
    section_index = lax.broadcasted_iota(jnp.int32, (SECTIONS, D, FF), 0)
    column = lax.broadcasted_iota(jnp.int32, (SECTIONS, D, FF), 2)
    boost = jnp.where((section_index % 2 == 0) & (column >= 3 * D), 8.0, 1.0)
    return base * boost * D ** (-0.5)


def draw_vec_master(key, part):
    key = jax.random.fold_in(key, 23)
    base = jnp.clip(jax.random.normal(key, (SECTIONS, VEC), jnp.float32), -4.0, 4.0)
    column = lax.broadcasted_iota(jnp.int32, (SECTIONS, VEC), 1)
    is_gain = (column >= FF) & (column < FF + D)
    return jnp.where(is_gain, 1.0 + 0.1 * base, 0.2 * base)


def levels(own_key, shape, cuts, low, top_value):
    level, own = 1.0, jax.random.fold_in(own_key, 6)
    for position, parts in cuts:
        draws = jnp.exp(jax.random.uniform(jax.random.fold_in(own, position), (parts,), jnp.float32, low / len(cuts), top_value / len(cuts)))
        level = level * jnp.repeat(draws, shape[position] // parts).reshape([-1 if axis == position else 1 for axis in range(len(shape))])
    return level


def normal_values(key, dims, deviation, most, shards=(), kind=jnp.bfloat16):
    values = jax.random.normal(key, dims, jnp.float32) * deviation
    if len(shards) > 0:
        values = levels(key, dims, shards, -0.22, 0.18) * values
    return jnp.clip(values, min=-most, max=most).astype(kind)


def setup_inputs(seed: int = 0) -> dict:
    arg_keys = jax.random.split(jax.random.key(seed), 12)
    return {
        "inputs": normal_values(arg_keys[0], (TOKENS, D), 1.0, 6.0, ((0, 8),)),
        "cotangent": normal_values(arg_keys[1], (TOKENS, D), 1.0, 6.0, ((0, 8),)),
        "in_master": draw_in_master(jax.random.fold_in(arg_keys[11], 71), 0),
        "in_first": normal_values(arg_keys[3], (SECTIONS, D, FF), 10.0, 60.0, ((0, 4), (1, 8)), jnp.float32),
        "in_second": jnp.clip(jnp.exp(math.log(1000.0) - 4.6051702 * jax.random.uniform(arg_keys[4], (SECTIONS, D, FF), jnp.float32) ** levels(arg_keys[4], (SECTIONS, D, FF), ((0, 4), (1, 8)), -0.2, 0.2)), 10.0, 1000.0),
        "down_master": normal_values(arg_keys[5], (SECTIONS, FF // 2, D), FF ** -0.5, 0.109375, ((0, 4), (1, 8)), jnp.float32),
        "down_first": normal_values(arg_keys[6], (SECTIONS, FF // 2, D), 10.0, 60.0, ((0, 4), (1, 8)), jnp.float32),
        "down_second": jnp.clip(jnp.exp(math.log(1000.0) - 4.6051702 * jax.random.uniform(arg_keys[7], (SECTIONS, FF // 2, D), jnp.float32) ** levels(arg_keys[7], (SECTIONS, FF // 2, D), ((0, 4), (1, 8)), -0.2, 0.2)), 10.0, 1000.0),
        "vec_master": draw_vec_master(jax.random.fold_in(arg_keys[11], 71), 0),
        "vec_first": normal_values(arg_keys[9], (SECTIONS, VEC), 10.0, 60.0, ((0, 4), (1, 8)), jnp.float32),
        "vec_second": jnp.clip(jnp.exp(math.log(1000.0) - 4.6051702 * jax.random.uniform(arg_keys[10], (SECTIONS, VEC), jnp.float32) ** levels(arg_keys[10], (SECTIONS, VEC), ((0, 4), (1, 8)), -0.2, 0.2)), 10.0, 1000.0),
    }


@jax.custom_vjp
def low(v):
    return lax.optimization_barrier(v.astype(jnp.bfloat16)).astype(jnp.float32)

@jax.custom_vjp
def low_back(v):
    return v

def low_keep(v):
    return (low(v), None)

def low_pass(kept, grad):
    return (grad,)

def back_keep(v):
    return (v, None)

def back_low(kept, grad):
    return (low(grad),)
low.defvjp(low_keep, low_pass)
low_back.defvjp(back_keep, back_low)
HIGHEST_PRECISION = lax.Precision.HIGHEST
NORM_EPSILON = 1e-05
BETA_ONE = 0.9
BETA_TWO = 0.98
BIAS_ONE = 1.0 - 0.9 ** 10
BIAS_TWO = 1.0 - 0.98 ** 10
WEIGHT_DECAY = 0.01
ADAM_EPSILON = 1e-06

def product(former, latter):
    return jnp.dot(former, latter, precision=HIGHEST_PRECISION, preferred_element_type=jnp.float32)

def layer_norm(summed, norm_gain, norm_bias):
    average = lax.optimization_barrier(jnp.mean(summed, axis=-1, keepdims=True))
    centered = summed - average
    variance = lax.optimization_barrier(jnp.mean(centered * centered, axis=-1, keepdims=True))
    return centered * lax.rsqrt(variance + NORM_EPSILON) * norm_gain + norm_bias

def attention_block(hidden, weight, vector):
    bias_qkv = jnp.concatenate([vector[:D], jnp.zeros((D,), jnp.float32), vector[D:2 * D]])
    mixing = low(low_back(product(hidden, weight[:, :3 * D]) + bias_qkv))
    grouped = mixing.reshape(-1, SEQ, 3, HEADS, HEAD_DIM)
    queries = grouped[:, :, 0]
    key_rows = grouped[:, :, 1]
    value_rows = grouped[:, :, 2]
    scores = low_back(jnp.einsum('bqhd,bkhd->bhqk', queries, key_rows, precision=HIGHEST_PRECISION) * HEAD_DIM ** (-0.5))
    chances = low(jax.nn.softmax(scores, axis=-1))
    context = jnp.einsum('bhqk,bkhd->bqhd', chances, value_rows, precision=HIGHEST_PRECISION)
    context = low(low_back(context.reshape(hidden.shape[0], D)))
    branch = low_back(product(context, weight[:, 3 * D:])) + vector[2 * D:3 * D]
    return layer_norm(hidden + branch, vector[FF:FF + D], vector[FF + D:])

def feed_block(hidden, w_up, up_bias, w_down, down_bias, norm_gain, norm_bias):
    before = low_back(product(hidden, w_up) + up_bias)
    active = low(jax.nn.gelu(before, approximate=False))
    branch = low_back(product(active, w_down)) + down_bias
    return layer_norm(hidden + branch, norm_gain, norm_bias)

def run_group(sequence, probes, in_low, down_low, vectors):
    hidden = low_back(sequence + probes[0])
    section_values = []
    for layer_index in range(LAYERS):
        attend_section = 2 * layer_index
        feed_section = attend_section + 1
        mixed_out = attention_block(hidden, in_low[attend_section], vectors[attend_section])
        hidden = low(low_back(mixed_out + probes[feed_section]))
        section_values.append(hidden)
        w_down = jnp.concatenate([down_low[attend_section], down_low[feed_section]], axis=0)
        feed_out = feed_block(hidden, in_low[feed_section], vectors[feed_section][:FF], w_down, vectors[attend_section][3 * D:FF], vectors[feed_section][FF:FF + D], vectors[feed_section][FF + D:])
        if layer_index + 1 < LAYERS:
            hidden = low(low_back(feed_out + probes[feed_section + 1]))
        else:
            hidden = low(low_back(feed_out))
        section_values.append(hidden)
    return jnp.stack(section_values)

def forward(sequences, probes, in_master, down_master, vec_master):
    in_low = low(in_master)
    down_low = low(down_master)

    def group(carried, pieces):
        return (carried, run_group(pieces[0], pieces[1], in_low, down_low, vec_master))
    unused, section_values = lax.scan(jax.checkpoint(group), jnp.zeros((), jnp.float32), (sequences, probes))
    return (section_values[:, SECTIONS - 1], section_values)

def adam_update(master, first, second, gradient):
    first_new = BETA_ONE * first + (1.0 - BETA_ONE) * gradient
    second_new = BETA_TWO * second + (1.0 - BETA_TWO) * gradient * gradient
    update = first_new / BIAS_ONE / (jnp.sqrt(second_new / BIAS_TWO) + ADAM_EPSILON)
    return (update + WEIGHT_DECAY * master, first_new, second_new)

def reference(inputs, cotangent, in_master, in_first, in_second, down_master, down_first, down_second, vec_master, vec_first, vec_second):
    groups = TOKENS // SEQ
    sequences = inputs.astype(jnp.float32).reshape(groups, SEQ, D)
    probes = jnp.zeros((groups, SECTIONS, SEQ, D), jnp.float32)
    final_rows, pullback, section_values = jax.vjp(forward, sequences, probes, in_master, down_master, vec_master, has_aux=True)
    gradients = pullback(cotangent.astype(jnp.float32).reshape(groups, SEQ, D))
    section_outputs = section_values.transpose(1, 0, 2, 3).reshape(SECTIONS, TOKENS, D).astype(jnp.bfloat16)
    section_input_grads = gradients[1].transpose(1, 0, 2, 3).reshape(SECTIONS, TOKENS, D).astype(jnp.bfloat16)
    in_grad = gradients[2]
    down_grad = gradients[3]
    vec_grad = gradients[4]
    in_step, in_first_new, in_second_new = adam_update(in_master, in_first, in_second, in_grad)
    down_step, down_first_new, down_second_new = adam_update(down_master, down_first, down_second, down_grad)
    vec_step, vec_first_new, vec_second_new = adam_update(vec_master, vec_first, vec_second, vec_grad)
    return (section_outputs, section_input_grads, in_grad, down_grad, vec_grad, in_step, in_first_new, in_second_new, down_step, down_first_new, down_second_new, vec_step, vec_first_new, vec_second_new)
```

```python
import jax
import jax.numpy as jnp
from jax import lax
from jax.sharding import Mesh
from jax.sharding import PartitionSpec as P

D = 768
HEADS = 12
HEAD_DIM = 64
FF = 3072
SEQ = 512
VEC = 4608
HALF = D // 2
LANES = 384

NORM_EPSILON = 1e-05
BETA_ONE = 0.9
BETA_TWO = 0.98
BIAS_ONE = 1.0 - 0.9**10
BIAS_TWO = 1.0 - 0.98**10
WEIGHT_DECAY = 0.01
ADAM_EPSILON = 1e-06
ROOT_HALF = 0.7071067811865476
ROOT_TWO_PI = 2.5066282746310002
SCALE = HEAD_DIM**-0.5

AXES = ("dp", "x", "c")
LOW = jnp.bfloat16
WIDE = jnp.float32


def product(former, latter):
    return jnp.dot(former, latter, preferred_element_type=WIDE)


def inner_rows(former, latter):
    return lax.dot_general(former, latter, (((0,), (0,)), ((), ())), preferred_element_type=WIDE)


def outer_cols(former, latter):
    return lax.dot_general(former, latter, (((1,), (1,)), ((), ())), preferred_element_type=WIDE)


class Links:
    def __init__(self):
        self.count = lax.axis_size("dp")
        self.bits = self.count.bit_length() - 1
        self.dp = lax.axis_index("dp")
        self.x = lax.axis_index("x")
        self.c = lax.axis_index("c")

    def own(self, bit):
        if bit == "c":
            return self.c
        if bit == "x":
            return self.x
        return (self.dp >> bit) & 1

    def flip(self, value, bit):
        step = {"c": 1, "x": 2}.get(bit)
        if step is None:
            step = 4 << bit
        pairs = [(place, place ^ step) for place in range(4 * self.count)]
        return lax.ppermute(value, AXES, pairs)

    def axis(self, bit):
        return 0 if bit == "x" else self.bits - bit

    def gather(self, shard, order):
        held = shard.reshape((1,) * (self.bits + 1) + shard.shape)
        for bit in order:
            got = self.flip(held, bit)
            first = self.own(bit) == 0
            held = jnp.concatenate(
                [jnp.where(first, held, got), jnp.where(first, got, held)], axis=self.axis(bit)
            )
        return held.reshape((2, self.count) + shard.shape)

    def scatter(self, parts, order):
        held = parts.reshape((2,) * (self.bits + 1) + parts.shape[2:])
        for bit in order:
            own, axis = self.own(bit), self.axis(bit)
            kept = lax.dynamic_slice_in_dim(held, own, 1, axis)
            sent = lax.dynamic_slice_in_dim(held, 1 - own, 1, axis)
            got = self.flip(sent, bit)
            held = (kept.astype(WIDE) + got.astype(WIDE)).astype(parts.dtype)
        return held.reshape(parts.shape[2:])


def norm_forward(summed, norm_gain, norm_bias):
    average = jnp.mean(summed, axis=-1, keepdims=True)
    centered = summed - average
    variance = jnp.mean(centered * centered, axis=-1, keepdims=True)
    inverse_spread = lax.rsqrt(variance + NORM_EPSILON)
    normed = centered * inverse_spread
    return (normed * norm_gain + norm_bias).astype(LOW), normed, inverse_spread


def norm_backward(incoming, normed, inverse_spread, norm_gain):
    incoming = incoming.astype(WIDE)
    through = incoming * norm_gain
    summed_grad = inverse_spread * (
        through
        - jnp.mean(through, axis=-1, keepdims=True)
        - normed * jnp.mean(through * normed, axis=-1, keepdims=True)
    )
    return summed_grad, jnp.sum(incoming * normed, axis=0), jnp.sum(incoming, axis=0)


def attend_forward(links, hidden, w_qkv, w_out, bias_qkv, vector):
    rows = hidden.shape[0]
    mixing = (product(hidden, w_qkv) + bias_qkv).astype(LOW)
    queries, key_rows, value_rows = [
        mixing[:, i * HALF : (i + 1) * HALF].reshape(rows, HEADS // 2, HEAD_DIM) for i in range(3)
    ]
    scores = jnp.einsum("qhd,khd->hqk", queries, key_rows, preferred_element_type=WIDE) * SCALE
    chances = jax.nn.softmax(scores, axis=-1)
    context = jnp.einsum(
        "hqk,khd->qhd", chances.astype(LOW), value_rows, preferred_element_type=WIDE
    )
    context = context.reshape(rows, HALF).astype(LOW)
    part = product(context, w_out)
    branch = part + links.flip(part.astype(LOW), "c").astype(WIDE) + vector[2 * D : 3 * D]
    result, normed, spread = norm_forward(
        hidden.astype(WIDE) + branch, vector[FF : FF + D], vector[FF + D :]
    )
    return result, (hidden, queries, key_rows, value_rows, chances, context, normed, spread)


def feed_forward(links, hidden, w_up, w_down, bias_up, vector, nearby):
    before = product(hidden, w_up) + bias_up
    curve = 0.5 * (1.0 + lax.erf(before * ROOT_HALF))
    active = (before * curve).astype(LOW)
    slope = curve + before * jnp.exp(-0.5 * before * before) / ROOT_TWO_PI
    part = product(active, w_down)
    branch = part + links.flip(part.astype(LOW), "c").astype(WIDE) + nearby[3 * D : FF]
    result, normed, spread = norm_forward(
        hidden.astype(WIDE) + branch, vector[FF : FF + D], vector[FF + D :]
    )
    return result, (hidden, active, slope, normed, spread)


def attend_backward(links, incoming, saved, w_qkv, w_out, vector):
    hidden, queries, key_rows, value_rows, chances, context, normed, spread = saved
    rows = hidden.shape[0]
    summed_grad, gain_grad, bias_grad = norm_backward(
        incoming, normed, spread, vector[FF : FF + D]
    )
    branch_low = summed_grad.astype(LOW)
    out_grad = inner_rows(context, branch_low)
    context_grad = (
        outer_cols(branch_low, w_out).astype(LOW).reshape(rows, HEADS // 2, HEAD_DIM)
    )
    chance_grad = jnp.einsum(
        "qhd,khd->hqk", context_grad, value_rows, preferred_element_type=WIDE
    )
    score_grad = (
        chances * (chance_grad - jnp.sum(chances * chance_grad, axis=-1, keepdims=True))
    ).astype(LOW)
    query_grad = jnp.einsum("hqk,khd->qhd", score_grad, key_rows, preferred_element_type=WIDE)
    key_grad = jnp.einsum("hqk,qhd->khd", score_grad, queries, preferred_element_type=WIDE)
    value_grad = jnp.einsum(
        "hqk,qhd->khd", chances.astype(LOW), context_grad, preferred_element_type=WIDE
    )
    mixing_grad = jnp.concatenate(
        [
            (query_grad * SCALE).astype(LOW).reshape(rows, HALF),
            (key_grad * SCALE).astype(LOW).reshape(rows, HALF),
            value_grad.astype(LOW).reshape(rows, HALF),
        ],
        axis=1,
    )
    mixing_sum = jnp.sum(mixing_grad.astype(WIDE), axis=0)
    qkv_grad = inner_rows(hidden, mixing_grad)
    part = outer_cols(mixing_grad, w_qkv)
    hidden_grad = (
        summed_grad + part + links.flip(part.astype(LOW), "c").astype(WIDE)
    ).astype(LOW)
    return (
        hidden_grad,
        qkv_grad,
        out_grad,
        mixing_sum[:HALF],
        mixing_sum[2 * HALF :],
        jnp.sum(summed_grad, axis=0),
        gain_grad,
        bias_grad,
    )


def feed_backward(links, incoming, saved, w_up, w_down, vector):
    hidden, active, slope, normed, spread = saved
    summed_grad, gain_grad, bias_grad = norm_backward(
        incoming, normed, spread, vector[FF : FF + D]
    )
    branch_low = summed_grad.astype(LOW)
    down_grad = inner_rows(active, branch_low)
    before_grad = (outer_cols(branch_low, w_down) * slope).astype(LOW)
    up_grad = inner_rows(hidden, before_grad)
    part = outer_cols(before_grad, w_up)
    hidden_grad = (
        summed_grad + part + links.flip(part.astype(LOW), "c").astype(WIDE)
    ).astype(LOW)
    return (
        hidden_grad,
        down_grad,
        up_grad,
        jnp.sum(before_grad.astype(WIDE), axis=0),
        jnp.sum(summed_grad, axis=0),
        gain_grad,
        bias_grad,
    )


def adam_update(master, first, second, gradient):
    first_new = BETA_ONE * first + (1.0 - BETA_ONE) * gradient
    second_new = BETA_TWO * second + (1.0 - BETA_TWO) * gradient * gradient
    update = first_new / BIAS_ONE / (jnp.sqrt(second_new / BIAS_TWO) + ADAM_EPSILON)
    return (update + WEIGHT_DECAY * master, first_new, second_new)


def blocks_of(whole, rows):
    return whole.reshape(rows, 8, LANES).transpose(1, 0, 2)


def padded_rows(flat):
    rows = -(-flat.shape[-1] // LANES)
    rows = -(-rows // 16) * 16
    pad = [(0, 0)] * (flat.ndim - 1) + [(0, rows * LANES - flat.shape[-1])]
    return jnp.pad(flat, pad).reshape(flat.shape[:-1] + (rows, LANES))


def on_device(
    inputs,
    cotangent,
    in_master,
    in_first,
    in_second,
    down_master,
    down_first,
    down_second,
    vec_master,
    vec_first,
    vec_second,
):
    links = Links()
    count, x, c = links.count, links.x, links.c
    dp_bits = list(range(links.bits))[::-1]
    rows = D // count
    half_rows = rows // 2
    vec_part = VEC // count
    first_core = c == 0

    blocks = blocks_of(in_master[0].astype(LOW), rows)
    out_rows = blocks[6:8]
    sent = jnp.where(
        first_core,
        jnp.concatenate([blocks[1:6:2], out_rows[:, half_rows:].reshape(1, rows, LANES)]),
        blocks[:4],
    )
    kept = jnp.where(
        first_core,
        jnp.concatenate([blocks[0:6:2], out_rows[:, :half_rows].reshape(1, rows, LANES)]),
        blocks[4:],
    )
    vec_high = lax.reduce_precision(vec_master[0], 8, 7)
    vec_both = jnp.concatenate([vec_high, vec_master[0] - vec_high]).astype(LOW)
    vec_rows = padded_rows(vec_both)
    got = links.flip(
        jnp.concatenate([sent.reshape(4 * rows, LANES), vec_rows]), "c"
    )
    vec_got = got[4 * rows :]
    got = got[: 4 * rows].reshape(4, rows, LANES)
    attend_shard = jnp.where(first_core, kept, got)
    up_shard = jnp.where(first_core, got, kept)
    vec_shard = jnp.concatenate(
        [jnp.where(first_core, vec_rows, vec_got), jnp.where(first_core, vec_got, vec_rows)]
    )
    down_shard = down_master[0].astype(LOW)

    attend_all = links.gather(
        jnp.concatenate([attend_shard.reshape(4 * rows, LANES), vec_shard]), dp_bits + ["x"]
    )
    up_all = links.gather(up_shard.reshape(4 * rows, LANES), dp_bits[:-1] + ["x"] + dp_bits[-1:])
    down_all = links.gather(down_shard, dp_bits + ["x"])

    vec_all = attend_all[:, :, 4 * rows :].reshape(2, count, 2, -1)[..., : 2 * vec_part]
    vec_all = vec_all.reshape(2, count, 2, 2, vec_part).astype(WIDE)
    vec_all = (vec_all[:, :, :, 0] + vec_all[:, :, :, 1]).transpose(0, 2, 1, 3).reshape(2, 2, VEC)

    attend_all = attend_all[:, :, : 4 * rows].reshape(2, count, 4, rows, LANES)
    qkv_all = attend_all[:, :, :3].transpose(0, 1, 3, 2, 4).reshape(2, D, 3 * HALF)
    out_all = attend_all[:, :, 3].reshape(2, count, 2, half_rows, LANES)
    out_all = out_all.transpose(0, 1, 3, 2, 4).reshape(2, 2, count // 2, half_rows, D)
    out_own = jnp.where(first_core, out_all[:, 0], out_all[:, 1])
    out_got = links.flip(jnp.where(first_core, out_all[:, 1], out_all[:, 0]), "c")
    out_full = jnp.concatenate(
        [jnp.where(first_core, out_own, out_got), jnp.where(first_core, out_got, out_own)], axis=2
    ).reshape(2, HALF, D)
    up_full = up_all.reshape(2, count, 4, rows, LANES).transpose(0, 1, 3, 2, 4).reshape(2, D, FF // 2)
    down_full = down_all.reshape(2, FF // 2, D)

    def half_of(vector, start, width):
        return jnp.where(
            first_core, vector[start : start + width], vector[start + width : start + 2 * width]
        )

    hidden = lax.dynamic_slice_in_dim(inputs, x * SEQ, SEQ, 0)
    outputs, kept_parts = [], []
    for layer in range(2):
        attend_vec, feed_vec = vec_all[layer, 0], vec_all[layer, 1]
        bias_qkv = jnp.concatenate(
            [half_of(attend_vec, 0, HALF), jnp.zeros((HALF,), WIDE), half_of(attend_vec, D, HALF)]
        )
        hidden, saved = attend_forward(
            links, hidden, qkv_all[layer], out_full[layer], bias_qkv, attend_vec
        )
        outputs.append(hidden)
        kept_parts.append(saved)
        hidden, saved = feed_forward(
            links,
            hidden,
            up_full[layer],
            down_full[layer],
            half_of(feed_vec, 0, FF // 2),
            feed_vec,
            attend_vec,
        )
        outputs.append(hidden)
        kept_parts.append(saved)

    def to_sections(values):
        own = jnp.where(x == 0, *[jnp.where(first_core, values[2 * i], values[2 * i + 1]) for i in (0, 1)])
        away = jnp.where(x == 0, *[jnp.where(first_core, values[2 * i], values[2 * i + 1]) for i in (1, 0)])
        got = links.flip(away, "x")
        return jnp.concatenate([jnp.where(x == 0, own, got), jnp.where(x == 0, got, own)])[None]

    section_outputs = to_sections(outputs)

    def wide_half(value, width):
        zeros = jnp.zeros((width,), WIDE)
        return [jnp.where(first_core, value, zeros), jnp.where(first_core, zeros, value)]

    def scatter_rows(parts, order):
        n, lanes = parts.shape[1], parts.shape[3]
        split = parts.reshape(count, n, 2, half_rows, lanes).transpose(2, 0, 1, 3, 4)
        return links.scatter(split.reshape(2, count, n * half_rows, lanes), order)

    order_one = ["x"] + dp_bits[::-1]
    order_two = dp_bits[-1:] + ["x"] + dp_bits[:-1][::-1]
    grad = lax.dynamic_slice_in_dim(cotangent, x * SEQ, SEQ, 0)
    grads, vec_grads, sums = [None] * 4, [None] * 2, [None] * 2
    once = jnp.where(first_core, 1.0, 0.0)
    for layer in (1, 0):
        attend_vec, feed_vec = vec_all[layer, 0], vec_all[layer, 1]
        grad, down_grad, up_grad, up_sum, branch_sum, gain_sum, bias_sum = feed_backward(
            links, grad, kept_parts[2 * layer + 1], up_full[layer], down_full[layer], feed_vec
        )
        grads[2 * layer + 1] = grad
        down_sum = scatter_rows(down_grad.astype(LOW).reshape(count, 1, 2 * rows, D).reshape(count, 2, rows, D), order_one)
        up_sum_w = scatter_rows(
            up_grad.astype(LOW).reshape(count, rows, 4, LANES).transpose(0, 2, 1, 3), order_two
        )
        feed_grads = jnp.concatenate(
            wide_half(up_sum, FF // 2) + [once * gain_sum, once * bias_sum]
        )
        down_bias = once * branch_sum
        grad, qkv_grad, out_grad, query_sum, value_sum, branch_sum, gain_sum, bias_sum = (
            attend_backward(
                links, grad, kept_parts[2 * layer], qkv_all[layer], out_full[layer], attend_vec
            )
        )
        grads[2 * layer] = grad
        out_parts = out_grad.astype(LOW).reshape(count // 2, 2, half_rows, D)
        out_got = links.flip(jnp.where(first_core, out_parts[:, 1], out_parts[:, 0]), "c")
        out_own = jnp.where(first_core, out_parts[:, 0], out_parts[:, 1])
        out_parts = jnp.concatenate(
            [jnp.where(first_core, out_own, out_got), jnp.where(first_core, out_got, out_own)]
        )
        out_parts = out_parts.reshape(count, half_rows, 2, LANES).transpose(0, 2, 1, 3)
        attend_parts = jnp.concatenate(
            [
                qkv_grad.astype(LOW).reshape(count, rows, 3, LANES).transpose(0, 2, 1, 3),
                out_parts.reshape(count, 1, rows, LANES),
            ],
            axis=1,
        )
        attend_grads = jnp.concatenate(
            wide_half(query_sum, HALF)
            + wide_half(value_sum, HALF)
            + [once * branch_sum, down_bias, once * gain_sum, once * bias_sum]
        )
        vec_grads[layer] = (
            jnp.stack([attend_grads, feed_grads]).reshape(2, count, vec_part).transpose(1, 0, 2)
        )
        if layer:
            sums[layer] = [scatter_rows(attend_parts, order_two), up_sum_w, down_sum]
        else:
            split = attend_parts.reshape(count, 4, 2, half_rows, LANES).transpose(2, 0, 1, 3, 4)
            split = split.reshape(2, count, 4 * half_rows, LANES)
            vec_rows = padded_rows(jnp.stack(vec_grads).astype(LOW).reshape(2, count, -1))
            last = links.scatter(jnp.concatenate([split, vec_rows], axis=2), order_two)
            vec_last = last[4 * half_rows :]
            sums[layer] = [last[: 4 * half_rows], up_sum_w, down_sum]

    section_input_grads = to_sections(grads)

    flat = [jnp.concatenate([part.reshape(-1, LANES) for part in sums[i]]) for i in (0, 1)]
    own = jnp.where(x == 0, flat[0], flat[1])
    got = links.flip(jnp.where(x == 0, flat[1], flat[0]), "x")
    whole = [jnp.where(x == 0, own, got), jnp.where(x == 0, got, own)]
    n = 4 * half_rows
    both = [
        jnp.stack([w[i * n : (i + 1) * n].reshape(4, half_rows, LANES) for w in whole], axis=1).reshape(4, rows, LANES)
        for i in (0, 1)
    ]
    attend_sum, up_sum = both
    down_sum = jnp.stack(
        [w[2 * n :].reshape(2, half_rows, D) for w in whole], axis=1
    ).reshape(2 * rows, D)

    sent = jnp.where(first_core, up_sum, attend_sum).reshape(4 * rows, LANES)
    got = links.flip(jnp.concatenate([sent, vec_last]), "c")
    vec_got = got[4 * rows :]
    got = got[: 4 * rows].reshape(4, rows, LANES)
    kept = jnp.where(first_core, attend_sum, up_sum)

    def sides(part):
        return part.reshape(2, half_rows, LANES)

    attend_cols = [part for i in range(3) for part in (kept[i], got[i])] + [
        jnp.concatenate([sides(kept[3])[i], sides(got[3])[i]]) for i in (0, 1)
    ]
    up_cols = [got[i] for i in range(4)] + [kept[i] for i in range(4)]
    in_sum = jnp.concatenate(
        [jnp.where(first_core, a, u).astype(WIDE) for a, u in zip(attend_cols, up_cols)], axis=1
    )[None]
    down_sum = down_sum.astype(WIDE)[None]

    def vec_of(part):
        flat_vec = part.reshape(-1)[: 2 * vec_part].astype(WIDE)
        return jnp.where(first_core, flat_vec[:vec_part], flat_vec[vec_part:])

    vec_sum = (vec_of(vec_last) + vec_of(vec_got))[None]

    in_step, in_first_new, in_second_new = adam_update(in_master, in_first, in_second, in_sum)
    down_step, down_first_new, down_second_new = adam_update(
        down_master, down_first, down_second, down_sum
    )
    vec_step, vec_first_new, vec_second_new = adam_update(
        vec_master, vec_first, vec_second, vec_sum
    )
    return (
        section_outputs,
        section_input_grads,
        in_sum,
        down_sum,
        vec_sum,
        in_step,
        in_first_new,
        in_second_new,
        down_step,
        down_first_new,
        down_second_new,
        vec_step,
        vec_first_new,
        vec_second_new,
    )


def solution(mesh):
    grid = Mesh(mesh.devices.reshape(mesh.shape["dp"], 2, 2), AXES)
    tokens = P("dp", None)
    matrix = P(("x", "c"), "dp", None)
    vector = P(("x", "c"), "dp")
    return jax.shard_map(
        on_device,
        mesh=grid,
        in_specs=(tokens,) * 2 + (matrix,) * 6 + (vector,) * 3,
        out_specs=(matrix,) * 4 + (vector,) + (matrix,) * 6 + (vector,) * 3,
        check_vma=False,
    )
```

```python
import jax
import jax.numpy as jnp
from jax import lax
from jax.experimental import pallas as pl
from jax.experimental.pallas import tpu as pltpu
from jax.sharding import Mesh
from jax.sharding import PartitionSpec as P

D = 768
HEADS = 12
HEAD_DIM = 64
FF = 3072
SEQ = 512
VEC = 4608
HALF = D // 2
WIDTH = FF // 2
BLOCK = 128
STEP = 256
PAIR = 2 * HEAD_DIM

NORM_EPSILON = 1e-05
BETA_ONE = 0.9
BETA_TWO = 0.98
BIAS_ONE = 1.0 - 0.9**10
BIAS_TWO = 1.0 - 0.98**10
WEIGHT_DECAY = 0.01
ADAM_EPSILON = 1e-06
ROOT_HALF = 0.7071067811865476
ROOT_TWO_PI = 2.5066282746310002
SCALE = HEAD_DIM**-0.5

AXES = ("dp", "x", "c")
LOW = jnp.bfloat16
WIDE = jnp.float32


def mm(a, b):
    return lax.dot_general(a, b, (((1,), (0,)), ((), ())), preferred_element_type=WIDE)
def mm_cols(a, b):
    return lax.dot_general(a, b, (((1,), (1,)), ((), ())), preferred_element_type=WIDE)
def mm_rows(a, b):
    return lax.dot_general(a, b, (((0,), (0,)), ((), ())), preferred_element_type=WIDE)

def kernel_call(body, outs, ins, scratch=()):
    specs = [pl.BlockSpec(memory_space=pltpu.SMEM)] + [pl.BlockSpec(memory_space=pltpu.VMEM)] * (len(ins) - 1)
    return pl.pallas_call(
        body,
        out_shape=[jax.ShapeDtypeStruct(s, d) for s, d in outs],
        in_specs=specs,
        out_specs=[pl.BlockSpec(memory_space=pltpu.VMEM)] * len(outs),
        scratch_shapes=list(scratch),
        compiler_params=pltpu.CompilerParams(vmem_limit_bytes=48 * 2**20),
        cost_estimate=pl.CostEstimate(flops=1000, bytes_accessed=1000, transcendentals=0),
    )(*ins)

def norm_rows(total, vec, normed_ref, spread_ref, out_ref, rows):
    mean = jnp.mean(total, axis=-1, keepdims=True)
    centered = total - mean
    spread = lax.rsqrt(jnp.mean(centered * centered, axis=-1, keepdims=True) + NORM_EPSILON)
    normed = centered * spread
    normed_ref[rows, :] = normed.astype(LOW)
    spread_ref[rows, :] = spread
    out_ref[rows, :] = (normed * vec[4:5, :] + vec[5:6, :]).astype(LOW)

def joined_norm(before, own, got, bias, vec, normed, spread, out):
    def step(i, carry):
        rows = pl.ds(pl.multiple_of(i * BLOCK, BLOCK), BLOCK)
        total = before[rows, :].astype(WIDE) + own[rows, :].astype(WIDE) + got[rows, :].astype(WIDE) + bias
        norm_rows(total, vec, normed, spread, out, rows)
        return carry
    lax.fori_loop(0, SEQ // BLOCK, step, 0)

def half_row(place, row):
    return jnp.where(place[0] == 0, row[:, :HALF], row[:, HALF:])

NORM_OUTS = [((SEQ, D), LOW), ((SEQ, D), LOW), ((SEQ, 1), WIDE)]

def attend_body(place, hidden, w_qkv, w_out, vec, part, mixing, chances, context):
    bias = jnp.concatenate([half_row(place, vec[0:1, :]), jnp.zeros((1, HALF), WIDE), half_row(place, vec[1:2, :])], axis=1)
    for i in range(3):
        cols = slice(i * HALF, (i + 1) * HALF)
        mixing[:, cols] = (mm(hidden[...], w_qkv[:, cols]) + bias[:, cols]).astype(LOW)
    lane = lax.broadcasted_iota(jnp.int32, (SEQ, PAIR), 1)
    first = lane < HEAD_DIM
    for pair in range(HEADS // 4):
        at = pair * PAIR
        queries = mixing[:, at : at + PAIR] * jnp.asarray(SCALE, LOW)
        keys = mixing[:, HALF + at : HALF + at + PAIR]
        values = mixing[:, 2 * HALF + at : 2 * HALF + at + PAIR]
        sums = []
        for side in range(2):
            mine = first if side == 0 else ~first
            scores = mm_cols(jnp.where(mine, queries, jnp.zeros_like(queries)), keys)
            scores = jnp.exp(scores - jnp.max(scores, axis=-1, keepdims=True))
            low = (scores * (1.0 / jnp.sum(scores, axis=-1, keepdims=True))).astype(LOW)
            chances[2 * pair + side] = low
            sums.append(mm(low, values))
        context[:, at : at + PAIR] = jnp.where(first, sums[0], sums[1]).astype(LOW)
    for i in range(2):
        cols = slice(i * HALF, (i + 1) * HALF)
        part[:, cols] = mm(context[...], w_out[:, cols]).astype(LOW)

ATTEND_OUTS = [((SEQ, D), LOW), ((SEQ, 3 * HALF), LOW), ((HEADS // 2, SEQ, SEQ), LOW), ((SEQ, HALF), LOW)]

def attend_first(place, hidden, w_qkv, w_out, vec):
    return kernel_call(attend_body, ATTEND_OUTS, (place, hidden, w_qkv, w_out, vec))

def attend_next_body(place, before, own, got, feed_vec, last_vec, w_qkv, w_out, vec, hidden, normed, spread, *rest):
    joined_norm(before, own, got, last_vec[3:4, :], feed_vec, normed, spread, hidden)
    attend_body(place, hidden, w_qkv, w_out, vec, *rest)

def attend_next(place, before, own, got, feed_vec, last_vec, w_qkv, w_out, vec):
    return kernel_call(attend_next_body, NORM_OUTS + ATTEND_OUTS, (place, before, own, got, feed_vec, last_vec, w_qkv, w_out, vec))

def feed_body(place, before, own, got, vec, feed_vec, w_up, w_down, hidden, normed, spread, part, active, slope):
    joined_norm(before, own, got, vec[2:3, :], vec, normed, spread, hidden)
    for i in range(WIDTH // STEP):
        cols = slice(i * STEP, (i + 1) * STEP)
        row, col = divmod(i * STEP, D)
        bias = jnp.where(place[0] == 0, feed_vec[row : row + 1, col : col + STEP], feed_vec[row + 2 : row + 3, col : col + STEP])
        for j in range(2):
            rows = slice(j * SEQ // 2, (j + 1) * SEQ // 2)
            value = mm(hidden[rows, :], w_up[:, cols]) + bias
            curve = 0.5 * (1.0 + lax.erf(value * ROOT_HALF))
            active[rows, cols] = (value * curve).astype(LOW)
            slope[rows, cols] = (curve + value * jnp.exp(-0.5 * value * value) * (1.0 / ROOT_TWO_PI)).astype(LOW)
    for i in range(2):
        cols = slice(i * HALF, (i + 1) * HALF)
        part[:, cols] = mm(active[...], w_down[:, cols]).astype(LOW)

FEED_OUTS = NORM_OUTS + [((SEQ, D), LOW), ((SEQ, WIDTH), LOW), ((SEQ, WIDTH), LOW)]
def feed_forward(place, before, own, got, vec, feed_vec, w_up, w_down):
    return kernel_call(feed_body, FEED_OUTS, (place, before, own, got, vec, feed_vec, w_up, w_down))

def norm_backward(grad_rows, normed, spread, vec, summed, branch, sums, bias_row):
    def step(i, carry):
        rows = pl.ds(pl.multiple_of(i * BLOCK, BLOCK), BLOCK)
        grad = grad_rows(rows)
        n = normed[rows, :].astype(WIDE)
        through = grad * vec[4:5, :]
        out = spread[rows, :] * (
            through - jnp.mean(through, axis=-1, keepdims=True)
            - n * jnp.mean(through * n, axis=-1, keepdims=True))
        summed[rows, :] = out
        branch[rows, :] = out.astype(LOW)
        add = (jnp.sum(out, axis=0, keepdims=True), jnp.sum(grad * n, axis=0, keepdims=True), jnp.sum(grad, axis=0, keepdims=True))
        return tuple(a + b for a, b in zip(carry, add))
    zero = jnp.zeros((1, D), WIDE)
    return lax.fori_loop(0, SEQ // BLOCK, step, (zero, zero, zero))

def feed_back_core(place, grad_rows, normed, spread, feed_vec, w_up, w_down, slope, summed, branch, change, part, sums):
    once = jnp.where(place[0] == 0, 1.0, 0.0)
    branch_sum, gain_sum, bias_sum = norm_backward(grad_rows, normed, spread, feed_vec, summed, branch, sums, 0)
    sums[...] = jnp.zeros_like(sums)
    sums[4:5, :] = gain_sum * once
    sums[5:6, :] = bias_sum * once
    sums[6:7, :] = branch_sum * once
    for i in range(WIDTH // STEP):
        cols = slice(i * STEP, (i + 1) * STEP)
        row, col = divmod(i * STEP, D)
        total = jnp.zeros((1, STEP), WIDE)
        for j in range(2):
            rows = slice(j * SEQ // 2, (j + 1) * SEQ // 2)
            value = (mm_cols(branch[rows, :], w_down[cols, :]) * slope[rows, cols].astype(WIDE)).astype(LOW)
            change[rows, cols] = value
            total = total + jnp.sum(value.astype(WIDE), axis=0, keepdims=True)
        sums[row : row + 1, col : col + STEP] = total * once
        sums[row + 2 : row + 3, col : col + STEP] = total * (1.0 - once)
    for i in range(2):
        rows = slice(i * HALF, (i + 1) * HALF)
        part[:, rows] = mm_cols(change[...], w_up[rows, :]).astype(LOW)

BACK_OUTS = [((SEQ, D), WIDE), ((SEQ, D), LOW)]

def feed_last_body(place, before, own, got, last_vec, feed_vec, w_up, w_down, slope, cot, out, summed, branch, change, part, sums, normed, spread):
    joined_norm(before, own, got, last_vec[3:4, :], feed_vec, normed, spread, out)
    feed_back_core(place, lambda rows: cot[rows, :].astype(WIDE), normed, spread, feed_vec, w_up, w_down, slope, summed, branch, change, part, sums)

def feed_last(place, before, own, got, last_vec, feed_vec, w_up, w_down, slope, cot):
    return kernel_call(feed_last_body,
        [((SEQ, D), LOW)] + BACK_OUTS + [((SEQ, WIDTH), LOW), ((SEQ, D), LOW), ((8, D), WIDE)],
        (place, before, own, got, last_vec, feed_vec, w_up, w_down, slope, cot),
        [pltpu.VMEM((SEQ, D), LOW), pltpu.VMEM((SEQ, 1), WIDE)])

def joined_grad(before, own, got, grad):
    def rows_of(rows):
        value = (before[rows, :] + own[rows, :].astype(WIDE) + got[rows, :].astype(WIDE)).astype(LOW)
        grad[rows, :] = value
        return value.astype(WIDE)
    return rows_of

def feed_back_body(place, before, own, got, normed, spread, feed_vec, w_up, w_down, slope, grad, summed, branch, change, part, sums):
    feed_back_core(place, joined_grad(before, own, got, grad), normed, spread, feed_vec, w_up, w_down, slope, summed, branch, change, part, sums)

def feed_back(place, before, own, got, normed, spread, feed_vec, w_up, w_down, slope):
    return kernel_call(feed_back_body,
        [((SEQ, D), LOW)] + BACK_OUTS + [((SEQ, WIDTH), LOW), ((SEQ, D), LOW), ((8, D), WIDE)],
        (place, before, own, got, normed, spread, feed_vec, w_up, w_down, slope))

def attend_back_body(place, before, own, got, normed, spread, vec, w_qkv, w_out, mixing, chances, grad, summed, branch, change, part, sums, context_grad):
    once = jnp.where(place[0] == 0, 1.0, 0.0)
    branch_sum, gain_sum, bias_sum = norm_backward(joined_grad(before, own, got, grad), normed, spread, vec, summed, branch, sums, 2)
    sums[...] = jnp.zeros_like(sums)
    sums[2:3, :] = branch_sum * once
    sums[4:5, :] = gain_sum * once
    sums[5:6, :] = bias_sum * once
    context_grad[...] = mm_cols(branch[...], w_out[...]).astype(LOW)
    first = lax.broadcasted_iota(jnp.int32, (SEQ, PAIR), 1) < HEAD_DIM
    for pair in range(HEADS // 4):
        at = pair * PAIR
        queries = mixing[:, at : at + PAIR]
        keys = mixing[:, HALF + at : HALF + at + PAIR]
        values = mixing[:, 2 * HALF + at : 2 * HALF + at + PAIR]
        outer = context_grad[:, at : at + PAIR]
        parts = []
        for side in range(2):
            mine = first if side == 0 else ~first
            low = chances[2 * pair + side]
            change_c = mm_cols(jnp.where(mine, outer, jnp.zeros_like(outer)), values)
            weight = low.astype(WIDE)
            product = weight * change_c
            scores = (product - weight * jnp.sum(product, axis=-1, keepdims=True)).astype(LOW)
            parts.append((mm(scores, keys), mm_rows(scores, queries), mm_rows(low, outer)))
        for i, scale in ((0, SCALE), (1, SCALE), (2, 1.0)):
            cols = slice(i * HALF + at, i * HALF + at + PAIR)
            value = (jnp.where(first, parts[0][i], parts[1][i]) * scale).astype(LOW)
            change[:, cols] = value
            if i != 1:
                total = jnp.sum(value.astype(WIDE), axis=0, keepdims=True)
                row = i // 2
                sums[row : row + 1, at : at + PAIR] = total * once
                sums[row : row + 1, HALF + at : HALF + at + PAIR] = total * (1.0 - once)
    for i in range(2):
        rows = slice(i * HALF, (i + 1) * HALF)
        part[:, rows] = mm_cols(change[...], w_qkv[rows, :]).astype(LOW)

def attend_back(place, before, own, got, normed, spread, vec, w_qkv, w_out, mixing, chances):
    return kernel_call(attend_back_body,
        [((SEQ, D), LOW)] + BACK_OUTS + [((SEQ, 3 * HALF), LOW), ((SEQ, D), LOW), ((8, D), WIDE)],
        (place, before, own, got, normed, spread, vec, w_qkv, w_out, mixing, chances),
        [pltpu.VMEM((SEQ, HALF), LOW)])


def source_rows(place, bits, rows):
    starts = []
    for relative in range(1 << len(bits)):
        dp_mask = x_mask = 0
        for i, bit in enumerate(bits):
            if (relative >> (len(bits) - 1 - i)) & 1:
                if bit == "x":
                    x_mask = 1
                else:
                    dp_mask |= 1 << bit
        start = ((place[1] ^ dp_mask) * 2 + (place[2] ^ x_mask)) * rows
        starts.append(pl.multiple_of(start, 16))
    return starts


def spread_rows(place, bits, whole, kept, sent):
    rows = whole.shape[0] >> len(bits)
    half = 1 << (len(bits) - 1)
    for i, start in enumerate(source_rows(place, bits, rows)):
        target = kept if i < half else sent
        at = (i % half) * rows
        target[at : at + rows, :] = whole[pl.ds(start, rows), :]


def feed_weights_grad(place, active, branch, hidden, change, bits_down, bits_up):
    chips = 1 << len(bits_down)
    if (D // chips) % 16:
        plain = lambda a, b: mm_rows(a, b).astype(LOW)
        return plain(active, branch), plain(hidden, change)

    def body(place, active, branch, hidden, change, down_kept, down_sent, up_kept, up_sent, down, up):
        for i in range(WIDTH // HALF):
            rows = slice(i * HALF, (i + 1) * HALF)
            down[rows, :] = mm_rows(active[:, rows], branch[...]).astype(LOW)
        spread_rows(place, bits_down, down, down_kept, down_sent)
        for i in range(WIDTH // HALF):
            cols = slice(i * HALF, (i + 1) * HALF)
            up[:, cols] = mm_rows(hidden[...], change[:, cols]).astype(LOW)
        spread_rows(place, bits_up, up, up_kept, up_sent)

    down = kernel_call(
        body,
        [((WIDTH // 2, D), LOW)] * 2 + [((D // 2, WIDTH), LOW)] * 2,
        (place, active, branch, hidden, change),
        [pltpu.VMEM((WIDTH, D), LOW), pltpu.VMEM((D, WIDTH), LOW)],
    )
    return down[:2], down[2:]


def out_weight_grad(place, count, context, branch):
    rows = D // count
    if (rows // 2) % 16:
        parts = mm_rows(context, branch).astype(LOW).reshape(count // 2, 2, rows // 2, 2, HALF)
        parts = parts.transpose(1, 0, 3, 2, 4).reshape(2, count // 2, rows, HALF)
        first = place[0] == 0
        return jnp.where(first, parts[0], parts[1]), jnp.where(first, parts[1], parts[0])

    def body(place, context, branch, own, other, whole):
        half = rows // 2
        whole[...] = mm_rows(context[...], branch[...]).astype(LOW)
        for j in range(count // 2):
            for target, core in ((own, place[0]), (other, 1 - place[0])):
                start = pl.multiple_of(j * rows + core * half, 16)
                target[j, :half, :] = whole[pl.ds(start, half), :HALF]
                target[j, half:, :] = whole[pl.ds(start, half), HALF:]

    return kernel_call(
        body,
        [((count // 2, rows, HALF), LOW)] * 2,
        (place, context, branch),
        [pltpu.VMEM((HALF, D), LOW)],
    )


def out_weight(place, count, own, got):
    rows = D // count
    half = rows // 2
    if half % 16:
        first = place[0] == 0
        own, got = [p.reshape(count // 2, 2, half, HALF) for p in (own, got)]
        both = jnp.stack([jnp.where(first, own, got), jnp.where(first, got, own)], axis=1)
        return both.transpose(0, 1, 3, 2, 4).reshape(HALF, D)

    def body(place, own, got, whole):
        for j in range(count // 2):
            for source, core in ((own, place[0]), (got, 1 - place[0])):
                start = pl.multiple_of(j * rows + core * half, 16)
                whole[pl.ds(start, half), :HALF] = source[j, :half, :]
                whole[pl.ds(start, half), HALF:] = source[j, half:, :]

    return kernel_call(body, [((HALF, D), LOW)], (place, own, got))[0]


def attend_weights_grad(place, count, hidden, change, out_own, out_got, bits, sums=None):
    rows = D // count
    extra = 0 if sums is None else 16

    def vec_rows(sums):
        attend, feed = [
            jnp.concatenate([part[...][:8] for part in pair], axis=0) for pair in (sums[::2], sums[1::2])
        ]
        row = lax.broadcasted_iota(jnp.int32, (16, 1), 0) % 8
        down = jnp.concatenate(
            [jnp.broadcast_to(part[...][6:7], (8, D)) for part in sums[1::2]], axis=0
        )
        return jnp.concatenate([jnp.where(row == 3, down, attend), feed], axis=1).astype(LOW)

    if (rows // 2) % 16:
        first = place[0] == 0
        out_parts = jnp.concatenate(
            [jnp.where(first, out_own, out_got), jnp.where(first, out_got, out_own)]
        )
        parts = mm_rows(hidden, change).astype(LOW).reshape(count, rows, 3 * HALF)
        whole = jnp.concatenate([parts, out_parts], axis=2).reshape(D, WIDTH)
        return whole if sums is None else (whole, vec_rows(sums))

    def body(place, hidden, change, out_own, out_got, *rest):
        *sums, kept, sent, whole = rest
        for i in range(3):
            cols = slice(i * HALF, (i + 1) * HALF)
            whole[:, cols] = mm_rows(hidden[...], change[:, cols]).astype(LOW)
        for source, core in ((out_own, place[0]), (out_got, 1 - place[0])):
            for j in range(count // 2):
                start = pl.multiple_of((core * (count // 2) + j) * rows, 16)
                whole[pl.ds(start, rows), 3 * HALF :] = source[j]
        spread_rows(place, bits, whole, kept, sent)
        if sums:
            sent[D // 2 :, :] = vec_rows(sums)

    return kernel_call(
        body,
        [((D // 2, WIDTH), LOW), ((D // 2 + extra, WIDTH), LOW)],
        (place, hidden, change, out_own, out_got) + tuple(sums or ()),
        [pltpu.VMEM((D, WIDTH), LOW)],
    )


class Links:
    def __init__(self):
        self.count = lax.axis_size("dp")
        self.bits = self.count.bit_length() - 1
        self.dp = lax.axis_index("dp")
        self.x = lax.axis_index("x")
        self.c = lax.axis_index("c")
        self.plain = (D // self.count // 2) % 16 != 0

    def own(self, bit):
        if bit == "c":
            return self.c
        if bit == "x":
            return self.x
        return (self.dp >> bit) & 1

    def flip(self, value, bit):
        step = {"c": 1, "x": 2}.get(bit)
        if step is None:
            step = 4 << bit
        pairs = [(place, place ^ step) for place in range(4 * self.count)]
        return lax.ppermute(value, AXES, pairs)

    def order(self, names):
        bits = {"x": ["x"], "y": [0], "1": [1], "2": list(range(self.bits))[:1:-1]}
        return [bit for name in names for bit in bits[name]]

    def gather(self, shards, names, also=None):
        orders = [self.order(name) for name in names]
        held = [shard.reshape((1,) * (self.bits + 1) + shard.shape) for shard in shards]

        def joined(held, got, bit):
            first = self.own(bit) == 0
            axis = 0 if bit == "x" else self.bits - bit
            return jnp.concatenate(
                [jnp.where(first, held, got), jnp.where(first, got, held)], axis=axis
            )

        for step in range(self.bits):
            got = [self.flip(h, order[step]) for h, order in zip(held, orders)]
            got, more = lax.optimization_barrier((got, self.flip(also, step)))
            also = (also.astype(WIDE) + more.astype(WIDE)).astype(LOW)
            held = [joined(h, g, order[step]) for h, g, order in zip(held, got, orders)]
        more = self.flip(also, "x")
        first = self.x == 0
        vectors = [jnp.where(first, also, more), jnp.where(first, more, also)]
        layers = []
        for one, order, shard in zip(held, orders, shards):
            bit = order[-1]
            if bit == "x":
                got = self.flip(one, bit)
                both = [jnp.where(first, one, got), jnp.where(first, got, one)]
            else:
                both = [joined(h, self.flip(h, bit), bit) for h in (one[:1], one[1:])]
            layers.append([part.reshape((self.count,) + shard.shape) for part in both])
        return layers, vectors

    def scatter(self, parts, names, extra=None):
        bits = self.order(names)
        if self.plain:
            return self.scatter_plain(parts, bits, extra)
        kept, sent = parts
        if extra is not None:
            extra = sent[kept.shape[0] :]
        for step, bit in enumerate(bits):
            got = self.flip(sent, bit)
            kept, sent, extra = add_rows(kept, got, extra, step == len(bits) - 1)
        return kept if extra is None else (kept, extra)

    def scatter_plain(self, parts, bits, extra):
        lanes = parts.shape[1]
        held = parts.reshape((2,) * (self.bits + 1) + (-1, lanes))
        for bit in bits:
            own, axis = self.own(bit), self.bits if bit == "x" else self.bits - 1 - bit
            kept = lax.dynamic_slice_in_dim(held, own, 1, axis)
            sent = lax.dynamic_slice_in_dim(held, 1 - own, 1, axis)
            if extra is None:
                got = self.flip(sent, bit)
            else:
                got = self.flip(jnp.concatenate([sent.reshape(-1, lanes), extra]), bit)
                split = got.shape[0] - extra.shape[0]
                extra = (extra.astype(WIDE) + got[split:].astype(WIDE)).astype(LOW)
                got = got[:split].reshape(sent.shape)
            held = (kept.astype(WIDE) + got.astype(WIDE)).astype(LOW)
        held = held.reshape(-1, lanes)
        return held if extra is None else (held, extra)


def add_rows(kept, got, extra, last):
    rows, lanes = kept.shape
    more = 0 if extra is None else extra.shape[0]
    half = rows if last else rows // 2

    def body(place, kept, got, *rest):
        total = lambda at, size: (
            kept[at : at + size, :].astype(WIDE) + got[at : at + size, :].astype(WIDE)
        ).astype(LOW)
        if more:
            extra_sum = (rest[0][...].astype(WIDE) + got[rows:, :].astype(WIDE)).astype(LOW)
            rest[-1][...] = extra_sum
            rest = rest[1:-1]
        rest[0][...] = total(0, half)
        if not last:
            rest[1][:half, :] = total(half, half)
            if more:
                rest[1][half:, :] = extra_sum

    outs = [((half, lanes), LOW)]
    if not last:
        outs.append(((half + more, lanes), LOW))
    if more:
        outs.append(((more, lanes), LOW))
    ins = (jnp.zeros((1,), jnp.int32), kept, got) + ((extra,) if more else ())
    results = list(kernel_call(body, outs, ins))
    extra = results.pop() if more else None
    return results[0], None if last else results[1], extra


def adam_update(master, first, second, gradient):
    first_new = BETA_ONE * first + (1.0 - BETA_ONE) * gradient
    second_new = BETA_TWO * second + (1.0 - BETA_TWO) * gradient * gradient
    update = first_new / BIAS_ONE / (jnp.sqrt(second_new / BIAS_TWO) + ADAM_EPSILON)
    return (update + WEIGHT_DECAY * master, first_new, second_new)


def on_device(
    inputs,
    cotangent,
    in_master,
    in_first,
    in_second,
    down_master,
    down_first,
    down_second,
    vec_master,
    vec_first,
    vec_second,
):
    links = Links()
    count, x, c = links.count, links.x, links.c
    rows = D // count
    half_rows = rows // 2
    vec_part = VEC // count
    first_core = c == 0
    first_chip = x == 0
    place = jnp.stack([c, links.dp, x]).astype(jnp.int32)

    def mine(one, other):
        return jnp.where(first_core, one, other)

    def trade(part):
        return links.flip(part, "c")

    in_low = in_master[0].astype(LOW)
    out_rows = in_low[:, 3 * D :]
    pieces = []
    for core in (0, 1):
        out_half = out_rows[core * half_rows : (core + 1) * half_rows]
        pieces.append(
            jnp.concatenate(
                [in_low[:, i * D + core * HALF : i * D + (core + 1) * HALF] for i in range(3)]
                + [jnp.concatenate([out_half[:, :HALF], out_half[:, HALF:]], axis=0)],
                axis=1,
            )
        )
    got = trade(mine(pieces[1], in_low[:, :WIDTH]))
    attend_shard = mine(pieces[0], got)
    up_shard = mine(got, in_low[:, WIDTH:])
    down_shard = down_master[0].astype(LOW)

    placed = lax.dynamic_update_slice(
        jnp.zeros((VEC,), WIDE), vec_master[0], (links.dp * vec_part,)
    ).reshape(-1, D)
    high = lax.reduce_precision(placed, 8, 7)
    vec_both = jnp.pad(jnp.concatenate([high, placed - high]).astype(LOW), ((0, 4), (0, 0)))
    vec_got = trade(vec_both)
    vec_both = jnp.concatenate([mine(vec_both, vec_got), mine(vec_got, vec_both)])

    (attend_all, up_all, down_all), vectors = links.gather(
        [attend_shard, up_shard, down_shard], ["21xy", "2xy1", "2y1x"], vec_both
    )
    vecs, qkv, out, up, down = [], [], [], [], []
    for layer in (0, 1):
        vec = vectors[layer].astype(WIDE)
        vecs.append([vec[i : i + 6] + vec[i + 6 : i + 12] for i in (0, 16)])
        whole = attend_all[layer]
        qkv.append(whole[:, :, : 3 * HALF].reshape(D, 3 * HALF))
        parts = whole[:, :, 3 * HALF :].reshape(2, count // 2, rows, HALF)
        out.append(
            out_weight(place, count, mine(parts[0], parts[1]), trade(mine(parts[1], parts[0])))
        )
        up.append(up_all[layer].reshape(D, WIDTH))
        down.append(down_all[layer].reshape(WIDTH, D))

    hidden = [lax.dynamic_slice_in_dim(inputs, x * SEQ, SEQ, 0)]
    part, mixing_0, chances_0, context_0 = attend_first(
        place, hidden[0], qkv[0], out[0], vecs[0][0]
    )
    next_hidden, normed_0, spread_0, part, active_0, slope_0 = feed_forward(
        place, hidden[0], part, trade(part), vecs[0][0], vecs[0][1], up[0], down[0]
    )
    hidden.append(next_hidden)
    next_hidden, normed_1, spread_1, part, mixing_1, chances_1, context_1 = attend_next(
        place, hidden[1], part, trade(part), vecs[0][1], vecs[0][0], qkv[1], out[1], vecs[1][0]
    )
    hidden.append(next_hidden)
    next_hidden, normed_2, spread_2, part, active_1, slope_1 = feed_forward(
        place, hidden[2], part, trade(part), vecs[1][0], vecs[1][1], up[1], down[1]
    )
    hidden.append(next_hidden)

    def to_sections(values):
        low, high = mine(values[0], values[1]), mine(values[2], values[3])
        own = jnp.where(first_chip, low, high)
        got = links.flip(jnp.where(first_chip, high, low), "x")
        return jnp.concatenate(
            [jnp.where(first_chip, own, got), jnp.where(first_chip, got, own)]
        )[None]

    bits = {name: links.order(name) for name in ("x1y2", "1yx2", "yx21")}
    cotangent_rows = lax.dynamic_slice_in_dim(cotangent, x * SEQ, SEQ, 0)
    last, summed, branch, change, part, feed_sums_1 = feed_last(
        place, hidden[3], part, trade(part), vecs[1][0], vecs[1][1], up[1], down[1], slope_1, cotangent_rows
    )
    section_outputs = to_sections(hidden[1:] + [last])
    part_got = trade(part)
    down_parts_1, up_parts_1 = feed_weights_grad(
        place, active_1, branch, hidden[3], change, bits["x1y2"], bits["1yx2"]
    )
    down_sum_1 = links.scatter(down_parts_1, "x1y2")
    up_sum_1 = links.scatter(up_parts_1, "1yx2")
    grad_3, summed, branch, change, part, attend_sums_1 = attend_back(
        place, summed, part, part_got, normed_2, spread_2, vecs[1][0], qkv[1], out[1], mixing_1, chances_1
    )
    part_got = trade(part)
    out_own, out_other = out_weight_grad(place, count, context_1, branch)
    attend_parts = attend_weights_grad(
        place, count, hidden[2], change, out_own, trade(out_other), bits["yx21"]
    )
    attend_sum_1 = links.scatter(attend_parts, "yx21")
    grad_2, summed, branch, change, part, feed_sums_0 = feed_back(
        place, summed, part, part_got, normed_1, spread_1, vecs[0][1], up[0], down[0], slope_0
    )
    part_got = trade(part)
    down_parts_0, up_parts_0 = feed_weights_grad(
        place, active_0, branch, hidden[1], change, bits["x1y2"], bits["1yx2"]
    )
    down_sum_0 = links.scatter(down_parts_0, "x1y2")
    up_sum_0 = links.scatter(up_parts_0, "1yx2")
    grad_1, summed, branch, change, part, attend_sums_0 = attend_back(
        place, summed, part, part_got, normed_0, spread_0, vecs[0][0], qkv[0], out[0], mixing_0, chances_0
    )
    part_got = trade(part)
    out_own, out_other = out_weight_grad(place, count, context_0, branch)
    attend_parts = attend_weights_grad(
        place,
        count,
        hidden[0],
        change,
        out_own,
        trade(out_other),
        bits["yx21"],
        (attend_sums_0, feed_sums_0, attend_sums_1, feed_sums_1),
    )
    if links.plain:
        attend_sum_0, vec_total = links.scatter(attend_parts[0], "yx21", attend_parts[1])
    else:
        attend_sum_0, vec_total = links.scatter(attend_parts, "yx21", True)
    grad_0 = (summed + part.astype(WIDE) + part_got.astype(WIDE)).astype(LOW)
    section_input_grads = to_sections([grad_0, grad_1, grad_2, grad_3])

    whole = []
    for one, other in (
        (attend_sum_0, attend_sum_1),
        (up_sum_0, up_sum_1),
        (down_sum_0, down_sum_1),
    ):
        got = links.flip(jnp.where(first_chip, other, one), "x")
        own = jnp.where(first_chip, one, other)
        whole.append(
            jnp.concatenate([jnp.where(first_chip, own, got), jnp.where(first_chip, got, own)])
        )
    attend_sum, up_sum, down_sum = whole

    got = trade(jnp.concatenate([mine(up_sum, attend_sum), vec_total]))
    vec_total = vec_total.astype(WIDE) + got[rows:].astype(WIDE)
    got = got[:rows]
    kept = mine(attend_sum, up_sum)
    first, second = mine(kept, got), mine(got, kept)

    def joined(one, other):
        out_one, out_other = one[:, 3 * HALF :], other[:, 3 * HALF :]
        out_cols = [
            jnp.concatenate([out_one[i : i + half_rows], out_other[i : i + half_rows]])
            for i in (0, half_rows)
        ]
        cols = [part[:, i * HALF : (i + 1) * HALF] for i in range(3) for part in (one, other)]
        return jnp.concatenate(cols + out_cols, axis=1)

    in_sum = mine(joined(first, second), jnp.concatenate([first, second], axis=1))
    in_sum = in_sum.astype(WIDE)[None]
    down_sum = down_sum.astype(WIDE)[None]
    vec_sum = lax.dynamic_slice(vec_total, (8 * x, D * c), (6, D)).reshape(VEC)
    vec_sum = lax.dynamic_slice(vec_sum, (links.dp * vec_part,), (vec_part,))[None]

    in_step, in_first_new, in_second_new = adam_update(in_master, in_first, in_second, in_sum)
    down_step, down_first_new, down_second_new = adam_update(
        down_master, down_first, down_second, down_sum
    )
    vec_step, vec_first_new, vec_second_new = adam_update(
        vec_master, vec_first, vec_second, vec_sum
    )
    return (
        section_outputs,
        section_input_grads,
        in_sum,
        down_sum,
        vec_sum,
        in_step,
        in_first_new,
        in_second_new,
        down_step,
        down_first_new,
        down_second_new,
        vec_step,
        vec_first_new,
        vec_second_new,
    )


def solution(mesh):
    grid = Mesh(mesh.devices.reshape(mesh.shape["dp"], 2, 2), AXES)
    tokens = P("dp", None)
    matrix = P(("x", "c"), "dp", None)
    vector = P(("x", "c"), "dp")
    return jax.shard_map(
        on_device,
        mesh=grid,
        in_specs=(tokens,) * 2 + (matrix,) * 6 + (vector,) * 3,
        out_specs=(matrix,) * 4 + (vector,) + (matrix,) * 6 + (vector,) * 3,
        check_vma=False,
    )
```

```python
import jax
import jax.numpy as jnp
from jax import lax
from jax.experimental import pallas as pl
from jax.experimental.pallas import tpu as pltpu
from jax.sharding import Mesh
from jax.sharding import PartitionSpec as P

D = 768
HEADS = 12
HEAD_DIM = 64
FF = 3072
SEQ = 512
VEC = 4608
HALF = D // 2
WIDTH = FF // 2
BLOCK = 128
STEP = 256
PAIR = 2 * HEAD_DIM
VMEM_LIMIT = 14 * 2**20
FLOPS = 10**8
ORDER = "TWUtwuTUgWwutTGUWUW"

NORM_EPSILON = 1e-05
BETA_ONE = 0.9
BETA_TWO = 0.98
BIAS_ONE = 1.0 - 0.9**10
BIAS_TWO = 1.0 - 0.98**10
WEIGHT_DECAY = 0.01
ADAM_EPSILON = 1e-06
ROOT_HALF = 0.7071067811865476
ROOT_TWO_PI = 2.5066282746310002
SCALE = HEAD_DIM**-0.5

AXES = ("dp", "x", "c")
LOW = jnp.bfloat16
WIDE = jnp.float32


def mm(a, b):
    return lax.dot_general(a, b, (((1,), (0,)), ((), ())), preferred_element_type=WIDE)
def mm_cols(a, b):
    return lax.dot_general(a, b, (((1,), (1,)), ((), ())), preferred_element_type=WIDE)
def mm_rows(a, b):
    return lax.dot_general(a, b, (((0,), (0,)), ((), ())), preferred_element_type=WIDE)

class Weight:
    def __init__(self, shape, pieces, copies):
        self.shape, self.pieces, self.copies = shape, pieces, copies


class Arriving:
    def __init__(self, place, weight, refs, scratch, sem):
        self.scratch, self.sem, self.waiting = scratch, sem, True
        for source, row, condition in weight.copies(place, refs):
            copy = pltpu.make_async_copy(
                source, scratch.at[pl.ds(pl.multiple_of(row, 16), source.shape[0])], sem
            )
            if condition is None:
                copy.start()
            else:
                pl.when(condition)(copy.start)

    def __getitem__(self, at):
        if self.waiting:
            pltpu.make_async_copy(self.scratch, self.scratch, self.sem).wait()
            self.waiting = False
        return self.scratch[at]


def kernel_call(body, outs, ins, scratch=()):
    scratch = list(scratch)
    own_scratch = len(scratch)
    specs, flat = [], []
    for part in ins:
        if isinstance(part, Weight):
            specs += [pl.BlockSpec(memory_space=pl.ANY)] * len(part.pieces)
            flat += part.pieces
            scratch += [pltpu.VMEM(part.shape, LOW), pltpu.SemaphoreType.DMA]
        else:
            group = part if isinstance(part, tuple) else (part,)
            space = pltpu.VMEM if flat else pltpu.SMEM
            specs += [pl.BlockSpec(memory_space=space)] * len(group)
            flat += group

    def whole_body(*refs):
        at = [0]

        def take(number):
            at[0] += number
            return list(refs[at[0] - number : at[0]])

        inputs = [
            take(len(part.pieces) if isinstance(part, Weight) else len(part))
            if isinstance(part, (Weight, tuple))
            else take(1)[0]
            for part in ins
        ]
        results = take(len(outs) + own_scratch)
        for i, part in enumerate(ins):
            if isinstance(part, Weight):
                inputs[i] = Arriving(inputs[0], part, inputs[i], *take(2))
        body(*inputs, *results)

    return pl.pallas_call(
        whole_body,
        out_shape=[jax.ShapeDtypeStruct(s, d) for s, d in outs],
        in_specs=specs,
        out_specs=[pl.BlockSpec(memory_space=pltpu.VMEM)] * len(outs),
        scratch_shapes=scratch,
        compiler_params=pltpu.CompilerParams(vmem_limit_bytes=VMEM_LIMIT),
        cost_estimate=pl.CostEstimate(flops=FLOPS, bytes_accessed=1000, transcendentals=0),
    )(*flat)


def norm_rows(total, vec, normed_ref, spread_ref, out_ref, rows):
    mean = jnp.mean(total, axis=-1, keepdims=True)
    centered = total - mean
    spread = lax.rsqrt(jnp.mean(centered * centered, axis=-1, keepdims=True) + NORM_EPSILON)
    normed = centered * spread
    normed_ref[rows, :] = normed.astype(LOW)
    spread_ref[rows, :] = spread
    out_ref[rows, :] = (normed * vec[4:5, :] + vec[5:6, :]).astype(LOW)

def joined_norm(before, own, got, bias, vec, normed, spread, out):
    for i in range(SEQ // BLOCK):
        rows = slice(i * BLOCK, (i + 1) * BLOCK)
        total = before[rows, :].astype(WIDE) + own[rows, :].astype(WIDE) + got[i][...].astype(WIDE) + bias
        norm_rows(total, vec, normed, spread, out, rows)

def half_row(place, row):
    return jnp.where(place[0] == 0, row[:, :HALF], row[:, HALF:])

NORM_OUTS = [((SEQ, D), LOW), ((SEQ, D), LOW), ((SEQ, 1), WIDE)]

def attend_body(place, hidden, w_qkv, w_out, vec, part, mixing, chances, context):
    bias = jnp.concatenate([half_row(place, vec[0:1, :]), jnp.zeros((1, HALF), WIDE), half_row(place, vec[1:2, :])], axis=1)
    for i in range(3):
        cols = slice(i * HALF, (i + 1) * HALF)
        mixing[:, cols] = (mm(hidden[...], w_qkv[:, cols]) + bias[:, cols]).astype(LOW)
    lane = lax.broadcasted_iota(jnp.int32, (SEQ, PAIR), 1)
    first = lane < HEAD_DIM
    for pair in range(HEADS // 4):
        at = pair * PAIR
        queries = mixing[:, at : at + PAIR] * jnp.asarray(SCALE, LOW)
        keys = mixing[:, HALF + at : HALF + at + PAIR]
        values = mixing[:, 2 * HALF + at : 2 * HALF + at + PAIR]
        sums = []
        for side in range(2):
            mine = first if side == 0 else ~first
            scores = mm_cols(jnp.where(mine, queries, jnp.zeros_like(queries)), keys)
            scores = jnp.exp(scores - jnp.max(scores, axis=-1, keepdims=True))
            low = (scores * (1.0 / jnp.sum(scores, axis=-1, keepdims=True))).astype(LOW)
            chances[2 * pair + side] = low
            sums.append(mm(low, values))
        context[:, at : at + PAIR] = jnp.where(first, sums[0], sums[1]).astype(LOW)
    for i in range(2):
        cols = slice(i * HALF, (i + 1) * HALF)
        part[:, cols] = mm(context[...], w_out[:, cols]).astype(LOW)

ATTEND_OUTS = [((SEQ, D), LOW), ((SEQ, 3 * HALF), LOW), ((HEADS // 2, SEQ, SEQ), LOW), ((SEQ, HALF), LOW)]

def attend_first(place, hidden, w_qkv, w_out, vec):
    return kernel_call(attend_body, ATTEND_OUTS, (place, hidden, w_qkv, w_out, vec))

def attend_next_body(place, before, own, got, feed_vec, last_vec, w_qkv, w_out, vec, hidden, normed, spread, *rest):
    joined_norm(before, own, got, last_vec[3:4, :], feed_vec, normed, spread, hidden)
    attend_body(place, hidden, w_qkv, w_out, vec, *rest)

def attend_next(place, before, own, got, feed_vec, last_vec, w_qkv, w_out, vec):
    return kernel_call(attend_next_body, NORM_OUTS + ATTEND_OUTS, (place, before, own, got, feed_vec, last_vec, w_qkv, w_out, vec))

def feed_body(place, before, own, got, vec, feed_vec, w_up, w_down, hidden, normed, spread, part, active, slope):
    joined_norm(before, own, got, vec[2:3, :], vec, normed, spread, hidden)
    for i in range(WIDTH // STEP):
        cols = slice(i * STEP, (i + 1) * STEP)
        row, col = divmod(i * STEP, D)
        bias = jnp.where(place[0] == 0, feed_vec[row : row + 1, col : col + STEP], feed_vec[row + 2 : row + 3, col : col + STEP])
        for j in range(2):
            rows = slice(j * SEQ // 2, (j + 1) * SEQ // 2)
            value = mm(hidden[rows, :], w_up[:, cols]) + bias
            curve = 0.5 * (1.0 + lax.erf(value * ROOT_HALF))
            active[rows, cols] = (value * curve).astype(LOW)
            slope[rows, cols] = (curve + value * jnp.exp(-0.5 * value * value) * (1.0 / ROOT_TWO_PI)).astype(LOW)
    for i in range(2):
        cols = slice(i * HALF, (i + 1) * HALF)
        part[:, cols] = mm(active[...], w_down[:, cols]).astype(LOW)

FEED_OUTS = NORM_OUTS + [((SEQ, D), LOW), ((SEQ, WIDTH), LOW), ((SEQ, WIDTH), LOW)]
def feed_forward(place, before, own, got, vec, feed_vec, w_up, w_down):
    return kernel_call(feed_body, FEED_OUTS, (place, before, own, got, vec, feed_vec, w_up, w_down))

def norm_backward(grad_rows, normed, spread, vec, summed, branch, sums, bias_row):
    totals = [jnp.zeros((1, D), WIDE)] * 3
    for i in range(SEQ // BLOCK):
        rows = slice(i * BLOCK, (i + 1) * BLOCK)
        grad = grad_rows(i, rows)
        n = normed[rows, :].astype(WIDE)
        through = grad * vec[4:5, :]
        out = spread[rows, :] * (
            through
            - jnp.mean(through, axis=-1, keepdims=True)
            - n * jnp.mean(through * n, axis=-1, keepdims=True)
        )
        summed[rows, :] = out
        branch[rows, :] = out.astype(LOW)
        terms = (out, grad * n, grad)
        totals = [t + jnp.sum(term, axis=0, keepdims=True) for t, term in zip(totals, terms)]
    return totals


def feed_back_core(place, grad_rows, normed, spread, feed_vec, w_up, w_down, slope, summed, branch, change, part, sums):
    once = jnp.where(place[0] == 0, 1.0, 0.0)
    branch_sum, gain_sum, bias_sum = norm_backward(grad_rows, normed, spread, feed_vec, summed, branch, sums, 0)
    sums[...] = jnp.zeros_like(sums)
    sums[4:5, :] = gain_sum * once
    sums[5:6, :] = bias_sum * once
    sums[6:7, :] = branch_sum * once
    for i in range(WIDTH // STEP):
        cols = slice(i * STEP, (i + 1) * STEP)
        row, col = divmod(i * STEP, D)
        total = jnp.zeros((1, STEP), WIDE)
        for j in range(2):
            rows = slice(j * SEQ // 2, (j + 1) * SEQ // 2)
            value = (mm_cols(branch[rows, :], w_down[cols, :]) * slope[rows, cols].astype(WIDE)).astype(LOW)
            change[rows, cols] = value
            total = total + jnp.sum(value.astype(WIDE), axis=0, keepdims=True)
        sums[row : row + 1, col : col + STEP] = total * once
        sums[row + 2 : row + 3, col : col + STEP] = total * (1.0 - once)
    for i in range(2):
        rows = slice(i * HALF, (i + 1) * HALF)
        part[:, rows] = mm_cols(change[...], w_up[rows, :]).astype(LOW)

BACK_OUTS = [((SEQ, D), WIDE), ((SEQ, D), LOW)]

def feed_last_body(place, before, own, got, last_vec, feed_vec, w_up, w_down, slope, cot, out, summed, branch, change, part, sums, normed, spread):
    joined_norm(before, own, got, last_vec[3:4, :], feed_vec, normed, spread, out)
    feed_back_core(place, lambda i, rows: cot[rows, :].astype(WIDE), normed, spread, feed_vec, w_up, w_down, slope, summed, branch, change, part, sums)

def feed_last(place, before, own, got, last_vec, feed_vec, w_up, w_down, slope, cot):
    return kernel_call(feed_last_body,
        [((SEQ, D), LOW)] + BACK_OUTS + [((SEQ, WIDTH), LOW), ((SEQ, D), LOW), ((8, D), WIDE)],
        (place, before, own, got, last_vec, feed_vec, w_up, w_down, slope, cot),
        [pltpu.VMEM((SEQ, D), LOW), pltpu.VMEM((SEQ, 1), WIDE)])

def joined_grad(before, own, got, grad):
    def rows_of(i, rows):
        value = (before[rows, :] + own[rows, :].astype(WIDE) + got[i][...].astype(WIDE)).astype(LOW)
        grad[rows, :] = value
        return value.astype(WIDE)
    return rows_of

def feed_back_body(place, before, own, got, normed, spread, feed_vec, w_up, w_down, slope, grad, summed, branch, change, part, sums):
    feed_back_core(place, joined_grad(before, own, got, grad), normed, spread, feed_vec, w_up, w_down, slope, summed, branch, change, part, sums)

def feed_back(place, before, own, got, normed, spread, feed_vec, w_up, w_down, slope):
    return kernel_call(feed_back_body,
        [((SEQ, D), LOW)] + BACK_OUTS + [((SEQ, WIDTH), LOW), ((SEQ, D), LOW), ((8, D), WIDE)],
        (place, before, own, got, normed, spread, feed_vec, w_up, w_down, slope))

def attend_back_body(place, before, own, got, normed, spread, vec, w_qkv, w_out, mixing, chances, grad, summed, branch, change, part, sums, context_grad):
    once = jnp.where(place[0] == 0, 1.0, 0.0)
    branch_sum, gain_sum, bias_sum = norm_backward(joined_grad(before, own, got, grad), normed, spread, vec, summed, branch, sums, 2)
    sums[...] = jnp.zeros_like(sums)
    sums[2:3, :] = branch_sum * once
    sums[4:5, :] = gain_sum * once
    sums[5:6, :] = bias_sum * once
    context_grad[...] = mm_cols(branch[...], w_out[...]).astype(LOW)
    first = lax.broadcasted_iota(jnp.int32, (SEQ, PAIR), 1) < HEAD_DIM
    for pair in range(HEADS // 4):
        at = pair * PAIR
        queries = mixing[:, at : at + PAIR]
        keys = mixing[:, HALF + at : HALF + at + PAIR]
        values = mixing[:, 2 * HALF + at : 2 * HALF + at + PAIR]
        outer = context_grad[:, at : at + PAIR]
        parts = []
        for side in range(2):
            mine = first if side == 0 else ~first
            low = chances[2 * pair + side]
            change_c = mm_cols(jnp.where(mine, outer, jnp.zeros_like(outer)), values)
            weight = low.astype(WIDE)
            product = weight * change_c
            scores = (product - weight * jnp.sum(product, axis=-1, keepdims=True)).astype(LOW)
            parts.append((mm(scores, keys), mm_rows(scores, queries), mm_rows(low, outer)))
        for i, scale in ((0, SCALE), (1, SCALE), (2, 1.0)):
            cols = slice(i * HALF + at, i * HALF + at + PAIR)
            value = (jnp.where(first, parts[0][i], parts[1][i]) * scale).astype(LOW)
            change[:, cols] = value
            if i != 1:
                total = jnp.sum(value.astype(WIDE), axis=0, keepdims=True)
                row = i // 2
                sums[row : row + 1, at : at + PAIR] = total * once
                sums[row : row + 1, HALF + at : HALF + at + PAIR] = total * (1.0 - once)
    for i in range(2):
        rows = slice(i * HALF, (i + 1) * HALF)
        part[:, rows] = mm_cols(change[...], w_qkv[rows, : 3 * HALF]).astype(LOW)

def attend_back(place, before, own, got, normed, spread, vec, w_qkv, w_out, mixing, chances):
    return kernel_call(attend_back_body,
        [((SEQ, D), LOW)] + BACK_OUTS + [((SEQ, 3 * HALF), LOW), ((SEQ, D), LOW), ((8, D), WIDE)],
        (place, before, own, got, normed, spread, vec, w_qkv, w_out, mixing, chances),
        [pltpu.VMEM((SEQ, HALF), LOW)])


def source_rows(place, bits, rows):
    starts = []
    for relative in range(1 << len(bits)):
        dp_mask = x_mask = 0
        for i, bit in enumerate(bits):
            if (relative >> (len(bits) - 1 - i)) & 1:
                if bit == "x":
                    x_mask = 1
                else:
                    dp_mask |= 1 << bit
        start = place[1] ^ dp_mask
        if "x" in bits:
            start = start * 2 + (place[2] ^ x_mask)
        start = start * rows
        starts.append(pl.multiple_of(start, 16))
    return starts


def spread_rows(place, bits, whole, kept, sent):
    rows = whole.shape[0] >> len(bits)
    half = 1 << (len(bits) - 1)
    for i, start in enumerate(source_rows(place, bits, rows)):
        target = kept if i < half else sent
        at = (i % half) * rows
        target[at : at + rows, :] = whole[pl.ds(start, rows), :]


def feed_weights_grad(place, active, branch, hidden, change, bits_down, bits_up):
    if (D >> len(bits_down)) % 16:
        plain = lambda a, b: mm_rows(a, b).astype(LOW)
        return plain(active, branch), plain(hidden, change)

    def body(place, active, branch, hidden, change, down_kept, down_sent, up_kept, up_sent, down, up):
        for i in range(WIDTH // HALF):
            rows = slice(i * HALF, (i + 1) * HALF)
            down[rows, :] = mm_rows(active[:, rows], branch[...]).astype(LOW)
        spread_rows(place, bits_down, down, down_kept, down_sent)
        for i in range(WIDTH // HALF):
            cols = slice(i * HALF, (i + 1) * HALF)
            up[:, cols] = mm_rows(hidden[...], change[:, cols]).astype(LOW)
        spread_rows(place, bits_up, up, up_kept, up_sent)

    down = kernel_call(
        body,
        [((WIDTH // 2, D), LOW)] * 2 + [((D // 2, WIDTH), LOW)] * 2,
        (place, active, branch, hidden, change),
        [pltpu.VMEM((WIDTH, D), LOW), pltpu.VMEM((D, WIDTH), LOW)],
    )
    return down[:2], down[2:]


def out_weight_grad(place, count, context, branch):
    rows = D // count
    if (rows // 2) % 16:
        parts = mm_rows(context, branch).astype(LOW).reshape(count // 2, 2, rows // 2, 2, HALF)
        parts = parts.transpose(1, 0, 3, 2, 4).reshape(2, count // 2, rows, HALF)
        first = place[0] == 0
        return jnp.where(first, parts[0], parts[1]), jnp.where(first, parts[1], parts[0])

    def body(place, context, branch, own, other, whole):
        half = rows // 2
        whole[...] = mm_rows(context[...], branch[...]).astype(LOW)
        for j in range(count // 2):
            for target, core in ((own, place[0]), (other, 1 - place[0])):
                start = pl.multiple_of(j * rows + core * half, 16)
                target[j, :half, :] = whole[pl.ds(start, half), :HALF]
                target[j, half:, :] = whole[pl.ds(start, half), HALF:]

    return kernel_call(
        body,
        [((count // 2, rows, HALF), LOW)] * 2,
        (place, context, branch),
        [pltpu.VMEM((HALF, D), LOW)],
    )


def out_weight(place, count, own, got):
    rows = D // count
    half = rows // 2
    if half % 16:
        first = place[0] == 0
        own, got = [p.reshape(count // 2, 2, half, HALF) for p in (own, got)]
        both = jnp.stack([jnp.where(first, own, got), jnp.where(first, got, own)], axis=1)
        return both.transpose(0, 1, 3, 2, 4).reshape(HALF, D)

    def body(place, own, got, whole):
        for i in range(count // 2):
            j = ((((place[1] >> 1) & 1) ^ (i >> 1)) << 1) | (i & 1)
            for source, core in ((own, place[0]), (got, 1 - place[0])):
                start = pl.multiple_of(j * rows + core * half, 16)
                whole[pl.ds(start, half), :HALF] = source[i, :half, :]
                whole[pl.ds(start, half), HALF:] = source[i, half:, :]

    return kernel_call(body, [((HALF, D), LOW)], (place, own, got))[0]


def attend_weights_grad(place, count, hidden, change, out_own, out_got, bits, sums=None):
    rows = D // count
    extra = 0 if sums is None else 16

    def vec_rows(sums):
        attend, feed = [
            jnp.concatenate([part[...][:8] for part in pair], axis=0) for pair in (sums[::2], sums[1::2])
        ]
        row = lax.broadcasted_iota(jnp.int32, (16, 1), 0) % 8
        down = jnp.concatenate(
            [jnp.broadcast_to(part[...][6:7], (8, D)) for part in sums[1::2]], axis=0
        )
        return jnp.concatenate([jnp.where(row == 3, down, attend), feed], axis=1).astype(LOW)

    if (rows // 2) % 16:
        first = place[0] == 0
        out_parts = jnp.concatenate(
            [jnp.where(first, out_own, out_got), jnp.where(first, out_got, out_own)]
        )
        parts = mm_rows(hidden, change).astype(LOW).reshape(count, rows, 3 * HALF)
        whole = jnp.concatenate([parts, out_parts], axis=2).reshape(D, WIDTH)
        return whole if sums is None else (whole, vec_rows(sums))

    def body(place, hidden, change, out_own, out_got, *rest):
        *sums, kept, sent, whole = rest
        for i in range(3):
            cols = slice(i * HALF, (i + 1) * HALF)
            whole[:, cols] = mm_rows(hidden[...], change[:, cols]).astype(LOW)
        for source, core in ((out_own, place[0]), (out_got, 1 - place[0])):
            for j in range(count // 2):
                start = pl.multiple_of((core * (count // 2) + j) * rows, 16)
                whole[pl.ds(start, rows), 3 * HALF :] = source[j]
        spread_rows(place, bits, whole, kept, sent)
        if sums:
            sent[D // 2 :, :] = vec_rows(sums)

    return kernel_call(
        body,
        [((D // 2, WIDTH), LOW), ((D // 2 + extra, WIDTH), LOW)],
        (place, hidden, change, out_own, out_got) + tuple(sums or ()),
        [pltpu.VMEM((D, WIDTH), LOW)],
    )


class Links:
    def __init__(self):
        self.count = lax.axis_size("dp")
        self.bits = self.count.bit_length() - 1
        self.dp = lax.axis_index("dp")
        self.x = lax.axis_index("x")
        self.c = lax.axis_index("c")
        self.plain = (D // self.count // 2) % 16 != 0

    def own(self, bit):
        if bit == "c":
            return self.c
        if bit == "x":
            return self.x
        return (self.dp >> bit) & 1

    def flip(self, value, bit):
        step = {"c": 1, "x": 2}.get(bit)
        if step is None:
            step = 4 << bit
        pairs = [(place, place ^ step) for place in range(4 * self.count)]
        return lax.ppermute(value, AXES, pairs)

    def order(self, names):
        bits = {"x": ["x"], "y": [0], "1": [1], "2": list(range(self.bits))[:1:-1]}
        return [bit for name in names for bit in bits[name]]

class Gather:
    def __init__(self, links, shard, names):
        self.links, self.shape = links, shard.shape
        self.bits = links.order(names)
        self.held = shard.reshape((1,) * len(self.bits) + shard.shape)
        self.got = None
        self.layers = [None, None]

    def axis(self, bit):
        return 0 if bit == "x" else self.links.bits - bit

    def joined(self, held, got, bit):
        first = self.links.own(bit) == 0
        return jnp.concatenate(
            [jnp.where(first, held, got), jnp.where(first, got, held)], axis=self.axis(bit)
        )

    def send(self):
        bit = self.bits[0]
        if len(self.bits) > 1 or bit == "x":
            self.got = self.links.flip(self.held, bit)
        else:
            first = self.links.flip(self.held[:1], bit)
            self.got = [first, self.links.flip(tie(self.held[1:], first), bit)]

    def join(self):
        held = self.held
        self.held = self.joined(held, self.got, self.bits[0])
        self.bits = self.bits[1:]

    def whole(self, layer):
        if self.bits[0] == "x":
            whole = jnp.where(self.links.x == layer, self.held, self.got)
        else:
            whole = self.joined(self.held[layer : layer + 1], self.got[layer], self.bits[0])
        return whole.reshape((self.links.count,) + self.shape)

    def pieces(self, layer):
        if self.bits[0] == "x":
            return [part.reshape((-1,) + self.shape) for part in (self.held, self.got)]
        return [
            part.reshape((-1,) + self.shape) for part in (self.held[layer : layer + 1], self.got[layer])
        ]

    def weight(self, layer, rows, lanes):
        if self.links.plain:
            return self.whole(layer).reshape(rows, lanes)
        bit, size = self.bits[0], self.shape[0]

        def copies(place, refs):
            if bit == "x":
                own = place[2] == layer
                for source, condition in zip(refs, (own, jnp.logical_not(own))):
                    for chip in range(source.shape[0]):
                        yield source.at[chip], chip * size, condition
            else:
                for side, source in enumerate(refs):
                    one = ((place[1] >> bit) & 1) ^ side
                    for i in range(source.shape[0]):
                        chip = ((i >> bit) << (bit + 1)) | (one << bit) | (i & ((1 << bit) - 1))
                        yield source.at[i], chip * size, None

        return Weight((rows, lanes), self.pieces(layer), copies)


class Spread:
    def __init__(self, links, value, names):
        self.links, self.held = links, value
        self.bits = links.order(names)

    def send(self):
        self.got = self.links.flip(self.held, self.bits[0])

    def join(self):
        held, got = self.held, self.got
        if self.bits[0] == "x":
            first = self.links.x == 0
            self.held = jnp.concatenate([jnp.where(first, held, got), jnp.where(first, got, held)])
        else:
            self.held = (held.astype(WIDE) + got.astype(WIDE)).astype(LOW)
        self.bits = self.bits[1:]


class Scatter:
    def __init__(self, links, parts, names, extra=None, pieces=()):
        self.links, self.bits = links, links.order(names)
        self.pieces = list(pieces) + [1] * len(self.bits)
        self.plain = links.plain
        self.extra = extra
        if self.plain:
            self.kept = parts
        else:
            self.kept, self.sent = parts
            if extra is not None:
                self.extra = self.sent[self.kept.shape[0] :]

    def send(self):
        if not self.plain:
            number = self.pieces.pop(0)
            size = self.kept.shape[0] // number
            cuts = [i * size for i in range(number)] + [self.sent.shape[0]]
            self.got = tuple(
                self.links.flip(self.sent[a:b], self.bits[0]) for a, b in zip(cuts, cuts[1:])
            )

    def add(self, token):
        if self.plain:
            if self.bits:
                self.add_plain(tie(self.kept, token))
            return self.kept
        kept = tie(self.kept, token)
        self.kept, self.sent, self.extra = add_rows(kept, self.got, self.extra, len(self.bits) == 1)
        self.bits = self.bits[1:]
        return self.kept

    def add_plain(self, parts):
        links, lanes = self.links, parts.shape[1]
        has_x = "x" in self.bits
        held = parts.reshape((2,) * (links.bits + has_x) + (-1, lanes))
        for bit in self.bits:
            own, axis = links.own(bit), links.bits if bit == "x" else links.bits - 1 - bit
            kept = lax.dynamic_slice_in_dim(held, own, 1, axis)
            sent = lax.dynamic_slice_in_dim(held, 1 - own, 1, axis)
            if self.extra is None:
                got = links.flip(sent, bit)
            else:
                got = links.flip(jnp.concatenate([sent.reshape(-1, lanes), self.extra]), bit)
                split = got.shape[0] - self.extra.shape[0]
                self.extra = (self.extra.astype(WIDE) + got[split:].astype(WIDE)).astype(LOW)
                got = got[:split].reshape(sent.shape)
            held = (kept.astype(WIDE) + got.astype(WIDE)).astype(LOW)
        self.kept, self.bits = held.reshape(-1, lanes), []


def tie(value, token):
    return lax.optimization_barrier((value, token))[0]


def add_rows(kept, got, extra, last):
    rows, lanes = kept.shape
    more = 0 if extra is None else extra.shape[0]
    half = rows if last else rows // 2

    def body(place, kept, got, *rest):
        size = rows // len(got)
        if more:
            extra_sum = (rest[0][...].astype(WIDE) + got[-1][size:, :].astype(WIDE)).astype(LOW)
            rest[-1][...] = extra_sum
            rest = rest[1:-1]
            if not last:
                rest[1][half:, :] = extra_sum
        step = min(size, half)
        for at in range(0, rows, step):
            piece = got[at // size]
            start = at % size
            total = (
                kept[at : at + step, :].astype(WIDE) + piece[start : start + step, :].astype(WIDE)
            ).astype(LOW)
            target, to = (rest[0], at) if at < half else (rest[1], at - half)
            target[to : to + step, :] = total

    outs = [((half, lanes), LOW)]
    if not last:
        outs.append(((half + more, lanes), LOW))
    if more:
        outs.append(((more, lanes), LOW))
    ins = (jnp.zeros((1,), jnp.int32), kept, got) + ((extra,) if more else ())
    results = list(kernel_call(body, outs, ins))
    extra = results.pop() if more else None
    return results[0], None if last else results[1], extra


def adam_update(master, first, second, gradient):
    first_new = BETA_ONE * first + (1.0 - BETA_ONE) * gradient
    second_new = BETA_TWO * second + (1.0 - BETA_TWO) * gradient * gradient
    update = first_new / BIAS_ONE / (jnp.sqrt(second_new / BIAS_TWO) + ADAM_EPSILON)
    return (update + WEIGHT_DECAY * master, first_new, second_new)


def on_device(
    inputs,
    cotangent,
    in_master,
    in_first,
    in_second,
    down_master,
    down_first,
    down_second,
    vec_master,
    vec_first,
    vec_second,
):
    links = Links()
    count, x, c = links.count, links.x, links.c
    rows = D // count
    half_rows = rows // 2
    vec_part = VEC // count
    first_core = c == 0
    first_chip = x == 0
    place = jnp.stack([c, links.dp, x]).astype(jnp.int32)

    def mine(one, other):
        return jnp.where(first_core, one, other)

    def trade(part):
        return links.flip(part, "c")

    def trade_blocks(part):
        return tuple(trade(part[i : i + BLOCK]) for i in range(0, SEQ, BLOCK))

    in_low = in_master[0].astype(LOW)
    out_rows = in_low[:, 3 * D :]
    pieces = []
    for core in (0, 1):
        out_half = out_rows[core * half_rows : (core + 1) * half_rows]
        pieces.append(
            jnp.concatenate(
                [in_low[:, i * D + core * HALF : i * D + (core + 1) * HALF] for i in range(3)]
                + [jnp.concatenate([out_half[:, :HALF], out_half[:, HALF:]], axis=0)],
                axis=1,
            )
        )
    got = trade(mine(pieces[1], in_low[:, :WIDTH]))
    attend_shard = mine(pieces[0], got)
    up_shard = mine(got, in_low[:, WIDTH:])
    down_shard = down_master[0].astype(LOW)

    placed = lax.dynamic_update_slice(
        jnp.zeros((VEC,), WIDE), vec_master[0], (links.dp * vec_part,)
    ).reshape(-1, D)
    high = lax.reduce_precision(placed, 8, 7)
    vec_both = jnp.pad(jnp.concatenate([high, placed - high]).astype(LOW), ((0, 4), (0, 0)))
    vec_got = trade(vec_both)
    vec_both = jnp.concatenate([mine(vec_both, vec_got), mine(vec_got, vec_both)])

    small = Spread(links, vec_both, "yx21")
    attend_in = Gather(links, attend_shard, "2xy1")
    down_in = Gather(links, down_shard, "2y1x")
    up_in = Gather(links, up_shard, "12xy")
    streams = {"v": small, "t": attend_in, "w": down_in, "u": up_in}
    for name in "twu":
        streams[name].send()
    small.held = tie(small.held, attend_in.got)
    small.send()
    turns = "tvwuvtwuvtwvu" if links.bits == 3 else "twuv" * links.bits + "v"
    for name in turns:
        streams[name].join()
        if streams[name].bits:
            streams[name].send()
    vectors = small.held.reshape(2, 32, D)
    vecs = []
    for layer in (0, 1):
        vec = vectors[layer].astype(WIDE)
        vecs.append([vec[i : i + 6] + vec[i + 6 : i + 12] for i in (0, 16)])

    def attend_weights(layer):
        if links.plain:
            parts = attend_in.whole(layer)[None]
        else:
            parts = jnp.stack(attend_in.pieces(layer))
        parts = parts[..., 3 * HALF :].reshape(parts.shape[0], 2, -1, rows, HALF)
        own = mine(parts[:, 0], parts[:, 1]).reshape(-1, rows, HALF)
        got = trade(mine(parts[:, 1], parts[:, 0]).reshape(-1, rows, HALF))
        return attend_in.weight(layer, D, WIDTH), out_weight(place, count, own, got)

    qkv, out, up, down = [None] * 2, [None] * 2, [None] * 2, [None] * 2
    qkv[0], out[0] = attend_weights(0)
    hidden = [lax.dynamic_slice_in_dim(inputs, x * SEQ, SEQ, 0)]
    part, mixing_0, chances_0, context_0 = attend_first(
        place, hidden[0], qkv[0], out[0], vecs[0][0]
    )
    up[0] = up_in.weight(0, D, WIDTH)
    down[0] = down_in.weight(0, WIDTH, D)
    next_hidden, normed_0, spread_0, part, active_0, slope_0 = feed_forward(
        place, hidden[0], part, trade_blocks(part), vecs[0][0], vecs[0][1], up[0], down[0]
    )
    hidden.append(next_hidden)
    qkv[1], out[1] = attend_weights(1)
    next_hidden, normed_1, spread_1, part, mixing_1, chances_1, context_1 = attend_next(
        place, hidden[1], part, trade_blocks(part), vecs[0][1], vecs[0][0], qkv[1], out[1], vecs[1][0]
    )
    hidden.append(next_hidden)
    up[1] = up_in.weight(1, D, WIDTH)
    down[1] = down_in.weight(1, WIDTH, D)
    next_hidden, normed_2, spread_2, part, active_1, slope_1 = feed_forward(
        place, hidden[2], part, trade_blocks(part), vecs[1][0], vecs[1][1], up[1], down[1]
    )
    hidden.append(next_hidden)

    class Sections:
        def __init__(self, values):
            low, high = mine(values[0], values[1]), mine(values[2], values[3])
            self.own = jnp.where(first_chip, low, high)
            self.away = jnp.where(first_chip, high, low)

        def send(self, token):
            self.got = links.flip(tie(self.away, token), "x")

        def finish(self, token):
            own, got = tie(self.own, token), self.got
            self.whole = jnp.concatenate(
                [jnp.where(first_chip, own, got), jnp.where(first_chip, got, own)]
            )
            return self.whole

    def home(one, other):
        got = links.flip(jnp.where(first_chip, other, one), "x")
        own = jnp.where(first_chip, one, other)
        return jnp.concatenate(
            [jnp.where(first_chip, own, got), jnp.where(first_chip, got, own)]
        )

    names = {"w": "x1y2", "u": "1xy2", "t": "y12", "W": "xy12", "U": "1xy2"}
    bits = {name: links.order(order) for name, order in names.items()}

    def feed_sums(layer, active, branch, hidden, change):
        both = "wu" if layer else "WU"
        parts = feed_weights_grad(
            place, active, branch, hidden, change, bits[both[0]], bits[both[1]]
        )
        sums = [Scatter(links, part, names[name]) for part, name in zip(parts, both)]
        for each in sums:
            each.send()
        return sums

    def attend_sums(layer, context, branch, hidden, change, vector_sums=None):
        out_own, out_other = out_weight_grad(place, count, context, branch)
        parts = attend_weights_grad(
            place, count, hidden, change, out_own, trade(out_other), bits["t"], vector_sums
        )
        extra = None
        if vector_sums is not None:
            parts, extra = parts if links.plain else (parts, True)
        total = Scatter(links, parts, names["t"], extra)
        total.send()
        return total

    cotangent_rows = lax.dynamic_slice_in_dim(cotangent, x * SEQ, SEQ, 0)
    last, summed, branch, change, part, feed_vec_1 = feed_last(
        place, hidden[3], part, trade_blocks(part), vecs[1][0], vecs[1][1], up[1], down[1], slope_1, cotangent_rows
    )
    part_got = trade_blocks(part)
    outputs = Sections(hidden[1:] + [last])
    w_1, u_1 = feed_sums(1, active_1, branch, hidden[3], change)
    grad_3, summed, branch, change, part, attend_vec_1 = attend_back(
        place, tie(summed, u_1.kept), part, part_got, normed_2, spread_2, vecs[1][0], qkv[1], out[1], mixing_1, chances_1
    )
    part_got = trade_blocks(part)
    t_1 = attend_sums(1, context_1, branch, hidden[2], change)
    grad_2, summed, branch, change, part, feed_vec_0 = feed_back(
        place, tie(summed, t_1.kept), part, part_got, normed_1, spread_1, vecs[0][1], up[0], down[0], slope_0
    )
    part_got = trade_blocks(part)
    token = w_1.add(branch)
    w_1.send()
    token = u_1.add(token)
    u_1.send()
    w_0, u_0 = feed_sums(0, active_0, tie(branch, token), hidden[1], change)
    outputs.send(t_1.kept)
    token = outputs.finish(u_0.kept)
    grad_1, summed, branch, change, part, attend_vec_0 = attend_back(
        place, tie(summed, token), part, part_got, normed_0, spread_0, vecs[0][0], qkv[0], out[0], mixing_0, chances_0
    )
    part_got = trade_blocks(part)
    token = t_1.add(grad_1)
    t_1.send()
    token = w_1.add(token)
    w_1.send()
    token = u_1.add(token)
    u_1.send()
    t_0 = attend_sums(
        0,
        context_0,
        tie(branch, token),
        hidden[0],
        change,
        (attend_vec_0, feed_vec_0, attend_vec_1, feed_vec_1),
    )
    grad_0 = (summed + part.astype(WIDE) + jnp.concatenate(part_got).astype(WIDE)).astype(LOW)
    grads = Sections([grad_0, grad_1, grad_2, grad_3])
    token = t_0.kept
    sums = {"w": w_1, "u": u_1, "t": t_1, "W": w_0, "U": u_0, "T": t_0}
    for name in ORDER:
        if name in "og":
            (outputs if name == "o" else grads).send(token)
        elif name in "OG":
            token = (outputs if name == "O" else grads).finish(token)
        else:
            token = sums[name].add(token)
            if sums[name].bits:
                sums[name].send()
            elif name == "T":
                sent = jnp.concatenate([jnp.where(first_chip, t_1.kept, t_0.kept), t_0.extra])
                last_got = links.flip(sent, "x")
    down_sum = home(w_0.kept, w_1.kept)
    up_sum = home(u_0.kept, u_1.kept)

    got = last_got
    attend_sum = jnp.where(first_chip, t_0.kept, t_1.kept).astype(WIDE) + got[:rows].astype(WIDE)
    attend_sum = attend_sum.astype(LOW)
    vec_total = (t_0.extra.astype(WIDE) + got[rows:].astype(WIDE)).astype(LOW)
    section_outputs, section_input_grads = outputs.whole[None], grads.whole[None]

    got = trade(jnp.concatenate([mine(up_sum, attend_sum), vec_total]))
    vec_total = vec_total.astype(WIDE) + got[rows:].astype(WIDE)
    got = got[:rows]
    kept = mine(attend_sum, up_sum)
    first, second = mine(kept, got), mine(got, kept)

    def joined(one, other):
        out_one, out_other = one[:, 3 * HALF :], other[:, 3 * HALF :]
        out_cols = [
            jnp.concatenate([out_one[i : i + half_rows], out_other[i : i + half_rows]])
            for i in (0, half_rows)
        ]
        cols = [part[:, i * HALF : (i + 1) * HALF] for i in range(3) for part in (one, other)]
        return jnp.concatenate(cols + out_cols, axis=1)

    in_sum = mine(joined(first, second), jnp.concatenate([first, second], axis=1))
    in_sum = in_sum.astype(WIDE)[None]
    down_sum = down_sum.astype(WIDE)[None]
    vec_sum = lax.dynamic_slice(vec_total, (8 * x, D * c), (6, D)).reshape(VEC)
    vec_sum = lax.dynamic_slice(vec_sum, (links.dp * vec_part,), (vec_part,))[None]

    in_step, in_first_new, in_second_new = adam_update(in_master, in_first, in_second, in_sum)
    down_step, down_first_new, down_second_new = adam_update(
        down_master, down_first, down_second, down_sum
    )
    vec_step, vec_first_new, vec_second_new = adam_update(
        vec_master, vec_first, vec_second, vec_sum
    )
    return (
        section_outputs,
        section_input_grads,
        in_sum,
        down_sum,
        vec_sum,
        in_step,
        in_first_new,
        in_second_new,
        down_step,
        down_first_new,
        down_second_new,
        vec_step,
        vec_first_new,
        vec_second_new,
    )


def solution(mesh):
    grid = Mesh(mesh.devices.reshape(mesh.shape["dp"], 2, 2), AXES)
    tokens = P("dp", None)
    matrix = P(("x", "c"), "dp", None)
    vector = P(("x", "c"), "dp")
    return jax.shard_map(
        on_device,
        mesh=grid,
        in_specs=(tokens,) * 2 + (matrix,) * 6 + (vector,) * 3,
        out_specs=(matrix,) * 4 + (vector,) + (matrix,) * 6 + (vector,) * 3,
        check_vma=False,
    )
```

```python
import jax
import jax.numpy as jnp
from jax import lax
from jax.experimental import pallas as pl
from jax.experimental.pallas import tpu as pltpu
from jax.sharding import Mesh
from jax.sharding import PartitionSpec as P

D = 768
HEADS = 12
HEAD_DIM = 64
FF = 3072
SEQ = 512
VEC = 4608
HALF = D // 2
WIDTH = FF // 2
BLOCK = 128
STEP = 256
PAIR = 2 * HEAD_DIM
VMEM_LIMIT = 14 * 2**20
FLOPS = 10**8
ORDER = "UWTtpgTUWtTPGqQ"

NORM_EPSILON = 1e-05
BETA_ONE = 0.9
BETA_TWO = 0.98
BIAS_ONE = 1.0 - 0.9**10
BIAS_TWO = 1.0 - 0.98**10
WEIGHT_DECAY = 0.01
ADAM_EPSILON = 1e-06
ROOT_HALF = 0.7071067811865476
ROOT_TWO_PI = 2.5066282746310002
SCALE = HEAD_DIM**-0.5

AXES = ("dp", "x", "c")
LOW = jnp.bfloat16
WIDE = jnp.float32


def mm(a, b):
    return lax.dot_general(a, b, (((1,), (0,)), ((), ())), preferred_element_type=WIDE)
def mm_cols(a, b):
    return lax.dot_general(a, b, (((1,), (1,)), ((), ())), preferred_element_type=WIDE)
def mm_rows(a, b):
    return lax.dot_general(a, b, (((0,), (0,)), ((), ())), preferred_element_type=WIDE)

class Weight:
    def __init__(self, shape, pieces, copies):
        self.shape, self.pieces, self.copies = shape, pieces, copies


class Arriving:
    def __init__(self, place, weight, refs, scratch, sem):
        self.scratch, self.sem, self.waiting = scratch, sem, True
        for source, row, condition in weight.copies(place, refs):
            copy = pltpu.make_async_copy(
                source, scratch.at[pl.ds(pl.multiple_of(row, 16), source.shape[0])], sem
            )
            if condition is None:
                copy.start()
            else:
                pl.when(condition)(copy.start)

    def __getitem__(self, at):
        if self.waiting:
            pltpu.make_async_copy(self.scratch, self.scratch, self.sem).wait()
            self.waiting = False
        return self.scratch[at]


def kernel_call(body, outs, ins, scratch=(), after=()):
    scratch = list(scratch)
    own_scratch = len(scratch)
    specs, flat = [], []
    for part in ins:
        if isinstance(part, Weight):
            specs += [pl.BlockSpec(memory_space=pl.ANY)] * len(part.pieces)
            flat += part.pieces
            scratch += [pltpu.VMEM(part.shape, LOW), pltpu.SemaphoreType.DMA]
        else:
            group = part if isinstance(part, tuple) else (part,)
            space = pltpu.VMEM if flat else pltpu.SMEM
            specs += [pl.BlockSpec(memory_space=space)] * len(group)
            flat += group

    specs += [pl.BlockSpec(memory_space=pl.ANY)] * len(after)
    flat += after

    def whole_body(*refs):
        at = [0]

        def take(number):
            at[0] += number
            return list(refs[at[0] - number : at[0]])

        inputs = [
            take(len(part.pieces) if isinstance(part, Weight) else len(part))
            if isinstance(part, (Weight, tuple))
            else take(1)[0]
            for part in ins
        ]
        take(len(after))
        results = take(len(outs) + own_scratch)
        for i, part in enumerate(ins):
            if isinstance(part, Weight):
                inputs[i] = Arriving(inputs[0], part, inputs[i], *take(2))
        body(*inputs, *results)

    return pl.pallas_call(
        whole_body,
        out_shape=[jax.ShapeDtypeStruct(s, d) for s, d in outs],
        in_specs=specs,
        out_specs=[pl.BlockSpec(memory_space=pltpu.VMEM)] * len(outs),
        scratch_shapes=scratch,
        compiler_params=pltpu.CompilerParams(vmem_limit_bytes=VMEM_LIMIT),
        cost_estimate=pl.CostEstimate(flops=FLOPS, bytes_accessed=1000, transcendentals=0),
    )(*flat)


def norm_rows(total, vec, normed_ref, spread_ref, out_ref, rows):
    mean = jnp.mean(total, axis=-1, keepdims=True)
    centered = total - mean
    spread = lax.rsqrt(jnp.mean(centered * centered, axis=-1, keepdims=True) + NORM_EPSILON)
    normed = centered * spread
    normed_ref[rows, :] = normed.astype(LOW)
    spread_ref[rows, :] = spread
    out_ref[rows, :] = (normed * vec[4:5, :] + vec[5:6, :]).astype(LOW)

def joined_norm(before, own, got, bias, vec, normed, spread, out):
    for i in range(SEQ // BLOCK):
        rows = slice(i * BLOCK, (i + 1) * BLOCK)
        total = before[rows, :].astype(WIDE) + own[rows, :].astype(WIDE) + got[i][...].astype(WIDE) + bias
        norm_rows(total, vec, normed, spread, out, rows)

def half_row(place, row):
    return jnp.where(place[0] == 0, row[:, :HALF], row[:, HALF:])

NORM_OUTS = [((SEQ, D), LOW), ((SEQ, D), LOW), ((SEQ, 1), WIDE)]

def attend_body(place, hidden, w_qkv, w_out, vec, part, mixing, chances, context):
    bias = jnp.concatenate([half_row(place, vec[0:1, :]), jnp.zeros((1, HALF), WIDE), half_row(place, vec[1:2, :])], axis=1)
    for i in range(3):
        cols = slice(i * HALF, (i + 1) * HALF)
        mixing[:, cols] = (mm(hidden[...], w_qkv[:, cols]) + bias[:, cols]).astype(LOW)
    lane = lax.broadcasted_iota(jnp.int32, (SEQ, PAIR), 1)
    first = lane < HEAD_DIM
    for pair in range(HEADS // 4):
        at = pair * PAIR
        queries = mixing[:, at : at + PAIR] * jnp.asarray(SCALE, LOW)
        keys = mixing[:, HALF + at : HALF + at + PAIR]
        values = mixing[:, 2 * HALF + at : 2 * HALF + at + PAIR]
        sums = []
        for side in range(2):
            mine = first if side == 0 else ~first
            scores = mm_cols(jnp.where(mine, queries, jnp.zeros_like(queries)), keys)
            scores = jnp.exp(scores - jnp.max(scores, axis=-1, keepdims=True))
            low = (scores * (1.0 / jnp.sum(scores, axis=-1, keepdims=True))).astype(LOW)
            chances[2 * pair + side] = low
            sums.append(mm(low, values))
        context[:, at : at + PAIR] = jnp.where(first, sums[0], sums[1]).astype(LOW)
    for i in range(2):
        cols = slice(i * HALF, (i + 1) * HALF)
        part[:, cols] = mm(context[...], w_out[:, cols]).astype(LOW)

ATTEND_OUTS = [((SEQ, D), LOW), ((SEQ, 3 * HALF), LOW), ((HEADS // 2, SEQ, SEQ), LOW), ((SEQ, HALF), LOW)]

def attend_first(place, hidden, w_qkv, w_out, vec):
    return kernel_call(attend_body, ATTEND_OUTS, (place, hidden, w_qkv, w_out, vec))

def attend_next_body(place, before, own, got, feed_vec, last_vec, w_qkv, w_out, vec, hidden, normed, spread, *rest):
    joined_norm(before, own, got, last_vec[3:4, :], feed_vec, normed, spread, hidden)
    attend_body(place, hidden, w_qkv, w_out, vec, *rest)

def attend_next(place, before, own, got, feed_vec, last_vec, w_qkv, w_out, vec):
    return kernel_call(attend_next_body, NORM_OUTS + ATTEND_OUTS, (place, before, own, got, feed_vec, last_vec, w_qkv, w_out, vec))

def feed_body(place, before, own, got, vec, feed_vec, w_up, w_down, hidden, normed, spread, part, active, slope):
    joined_norm(before, own, got, vec[2:3, :], vec, normed, spread, hidden)
    for i in range(WIDTH // STEP):
        cols = slice(i * STEP, (i + 1) * STEP)
        row, col = divmod(i * STEP, D)
        bias = jnp.where(place[0] == 0, feed_vec[row : row + 1, col : col + STEP], feed_vec[row + 2 : row + 3, col : col + STEP])
        for j in range(2):
            rows = slice(j * SEQ // 2, (j + 1) * SEQ // 2)
            value = mm(hidden[rows, :], w_up[:, cols]) + bias
            curve = 0.5 * (1.0 + lax.erf(value * ROOT_HALF))
            active[rows, cols] = (value * curve).astype(LOW)
            slope[rows, cols] = (curve + value * jnp.exp(-0.5 * value * value) * (1.0 / ROOT_TWO_PI)).astype(LOW)
    for i in range(2):
        cols = slice(i * HALF, (i + 1) * HALF)
        part[:, cols] = mm(active[...], w_down[:, cols]).astype(LOW)

FEED_OUTS = NORM_OUTS + [((SEQ, D), LOW), ((SEQ, WIDTH), LOW), ((SEQ, WIDTH), LOW)]
def feed_forward(place, before, own, got, vec, feed_vec, w_up, w_down):
    return kernel_call(feed_body, FEED_OUTS, (place, before, own, got, vec, feed_vec, w_up, w_down))

def norm_backward(grad_rows, normed, spread, vec, summed, branch, sums, bias_row):
    totals = [jnp.zeros((1, D), WIDE)] * 3
    for i in range(SEQ // BLOCK):
        rows = slice(i * BLOCK, (i + 1) * BLOCK)
        grad = grad_rows(i, rows)
        n = normed[rows, :].astype(WIDE)
        through = grad * vec[4:5, :]
        out = spread[rows, :] * (
            through
            - jnp.mean(through, axis=-1, keepdims=True)
            - n * jnp.mean(through * n, axis=-1, keepdims=True)
        )
        summed[rows, :] = out
        branch[rows, :] = out.astype(LOW)
        terms = (out, grad * n, grad)
        totals = [t + jnp.sum(term, axis=0, keepdims=True) for t, term in zip(totals, terms)]
    return totals


def feed_back_core(place, grad_rows, normed, spread, feed_vec, w_up, w_down, slope, summed, branch, change, part, sums):
    once = jnp.where(place[0] == 0, 1.0, 0.0)
    branch_sum, gain_sum, bias_sum = norm_backward(grad_rows, normed, spread, feed_vec, summed, branch, sums, 0)
    sums[...] = jnp.zeros_like(sums)
    sums[4:5, :] = gain_sum * once
    sums[5:6, :] = bias_sum * once
    sums[6:7, :] = branch_sum * once
    for i in range(WIDTH // STEP):
        cols = slice(i * STEP, (i + 1) * STEP)
        row, col = divmod(i * STEP, D)
        total = jnp.zeros((1, STEP), WIDE)
        for j in range(2):
            rows = slice(j * SEQ // 2, (j + 1) * SEQ // 2)
            value = (mm_cols(branch[rows, :], w_down[cols, :]) * slope[rows, cols].astype(WIDE)).astype(LOW)
            change[rows, cols] = value
            total = total + jnp.sum(value.astype(WIDE), axis=0, keepdims=True)
        sums[row : row + 1, col : col + STEP] = total * once
        sums[row + 2 : row + 3, col : col + STEP] = total * (1.0 - once)
    for i in range(2):
        rows = slice(i * HALF, (i + 1) * HALF)
        part[:, rows] = mm_cols(change[...], w_up[rows, :]).astype(LOW)

BACK_OUTS = [((SEQ, D), WIDE), ((SEQ, D), LOW)]

def feed_last_body(place, before, own, got, last_vec, feed_vec, w_up, w_down, slope, cot, out, summed, branch, change, part, sums, normed, spread):
    joined_norm(before, own, got, last_vec[3:4, :], feed_vec, normed, spread, out)
    feed_back_core(place, lambda i, rows: cot[rows, :].astype(WIDE), normed, spread, feed_vec, w_up, w_down, slope, summed, branch, change, part, sums)

def feed_last(place, before, own, got, last_vec, feed_vec, w_up, w_down, slope, cot):
    return kernel_call(feed_last_body,
        [((SEQ, D), LOW)] + BACK_OUTS + [((SEQ, WIDTH), LOW), ((SEQ, D), LOW), ((8, D), WIDE)],
        (place, before, own, got, last_vec, feed_vec, w_up, w_down, slope, cot),
        [pltpu.VMEM((SEQ, D), LOW), pltpu.VMEM((SEQ, 1), WIDE)])

def joined_grad(before, own, got, grad):
    def rows_of(i, rows):
        value = (before[rows, :] + own[rows, :].astype(WIDE) + got[i][...].astype(WIDE)).astype(LOW)
        grad[rows, :] = value
        return value.astype(WIDE)
    return rows_of

def feed_back_body(place, before, own, got, normed, spread, feed_vec, w_up, w_down, slope, grad, summed, branch, change, part, sums):
    feed_back_core(place, joined_grad(before, own, got, grad), normed, spread, feed_vec, w_up, w_down, slope, summed, branch, change, part, sums)

def feed_back(place, before, own, got, normed, spread, feed_vec, w_up, w_down, slope):
    return kernel_call(feed_back_body,
        [((SEQ, D), LOW)] + BACK_OUTS + [((SEQ, WIDTH), LOW), ((SEQ, D), LOW), ((8, D), WIDE)],
        (place, before, own, got, normed, spread, feed_vec, w_up, w_down, slope))

def attend_back_body(place, before, own, got, normed, spread, vec, w_qkv, w_out, mixing, chances, grad, summed, branch, change, part, sums, context_grad):
    once = jnp.where(place[0] == 0, 1.0, 0.0)
    branch_sum, gain_sum, bias_sum = norm_backward(joined_grad(before, own, got, grad), normed, spread, vec, summed, branch, sums, 2)
    sums[...] = jnp.zeros_like(sums)
    sums[2:3, :] = branch_sum * once
    sums[4:5, :] = gain_sum * once
    sums[5:6, :] = bias_sum * once
    context_grad[...] = mm_cols(branch[...], w_out[...]).astype(LOW)
    first = lax.broadcasted_iota(jnp.int32, (SEQ, PAIR), 1) < HEAD_DIM
    for pair in range(HEADS // 4):
        at = pair * PAIR
        queries = mixing[:, at : at + PAIR]
        keys = mixing[:, HALF + at : HALF + at + PAIR]
        values = mixing[:, 2 * HALF + at : 2 * HALF + at + PAIR]
        outer = context_grad[:, at : at + PAIR]
        parts = []
        for side in range(2):
            mine = first if side == 0 else ~first
            low = chances[2 * pair + side]
            change_c = mm_cols(jnp.where(mine, outer, jnp.zeros_like(outer)), values)
            weight = low.astype(WIDE)
            product = weight * change_c
            scores = (product - weight * jnp.sum(product, axis=-1, keepdims=True)).astype(LOW)
            parts.append((mm(scores, keys), mm_rows(scores, queries), mm_rows(low, outer)))
        for i, scale in ((0, SCALE), (1, SCALE), (2, 1.0)):
            cols = slice(i * HALF + at, i * HALF + at + PAIR)
            value = (jnp.where(first, parts[0][i], parts[1][i]) * scale).astype(LOW)
            change[:, cols] = value
            if i != 1:
                total = jnp.sum(value.astype(WIDE), axis=0, keepdims=True)
                row = i // 2
                sums[row : row + 1, at : at + PAIR] = total * once
                sums[row : row + 1, HALF + at : HALF + at + PAIR] = total * (1.0 - once)
    for i in range(2):
        rows = slice(i * HALF, (i + 1) * HALF)
        part[:, rows] = mm_cols(change[...], w_qkv[rows, : 3 * HALF]).astype(LOW)

def attend_back(place, before, own, got, normed, spread, vec, w_qkv, w_out, mixing, chances, after=()):
    return kernel_call(attend_back_body,
        [((SEQ, D), LOW)] + BACK_OUTS + [((SEQ, 3 * HALF), LOW), ((SEQ, D), LOW), ((8, D), WIDE)],
        (place, before, own, got, normed, spread, vec, w_qkv, w_out, mixing, chances),
        [pltpu.VMEM((SEQ, HALF), LOW)], after)


def source_rows(place, bits, rows):
    starts = []
    for relative in range(1 << len(bits)):
        dp_mask = x_mask = 0
        for i, bit in enumerate(bits):
            if (relative >> (len(bits) - 1 - i)) & 1:
                if bit == "x":
                    x_mask = 1
                else:
                    dp_mask |= 1 << bit
        start = place[1] ^ dp_mask
        if "x" in bits:
            start = start * 2 + (place[2] ^ x_mask)
        start = start * rows
        starts.append(pl.multiple_of(start, 16))
    return starts


def spread_rows(place, bits, whole, kept, sent):
    rows = whole.shape[0] >> len(bits)
    half = 1 << (len(bits) - 1)
    for i, start in enumerate(source_rows(place, bits, rows)):
        target = kept if i < half else sent
        at = (i % half) * rows
        target[at : at + rows, :] = whole[pl.ds(start, rows), :]


def feed_weights_grad(place, active, branch, hidden, change, bits_down, bits_up):
    if (D >> len(bits_down)) % 16:
        plain = lambda a, b: mm_rows(a, b).astype(LOW)
        return plain(active, branch), plain(hidden, change)

    def body(place, active, branch, hidden, change, down_kept, down_sent, up_kept, up_sent, down, up):
        for i in range(WIDTH // HALF):
            rows = slice(i * HALF, (i + 1) * HALF)
            down[rows, :] = mm_rows(active[:, rows], branch[...]).astype(LOW)
        spread_rows(place, bits_down, down, down_kept, down_sent)
        for i in range(WIDTH // HALF):
            cols = slice(i * HALF, (i + 1) * HALF)
            up[:, cols] = mm_rows(hidden[...], change[:, cols]).astype(LOW)
        spread_rows(place, bits_up, up, up_kept, up_sent)

    down = kernel_call(
        body,
        [((WIDTH // 2, D), LOW)] * 2 + [((D // 2, WIDTH), LOW)] * 2,
        (place, active, branch, hidden, change),
        [pltpu.VMEM((WIDTH, D), LOW), pltpu.VMEM((D, WIDTH), LOW)],
    )
    return down[:2], down[2:]


def out_weight_grad(place, count, context, branch):
    rows = D // count
    if (rows // 2) % 16:
        parts = mm_rows(context, branch).astype(LOW).reshape(count // 2, 2, rows // 2, 2, HALF)
        parts = parts.transpose(1, 0, 3, 2, 4).reshape(2, count // 2, rows, HALF)
        first = place[0] == 0
        return jnp.where(first, parts[0], parts[1]), jnp.where(first, parts[1], parts[0])

    def body(place, context, branch, own, other, whole):
        half = rows // 2
        whole[...] = mm_rows(context[...], branch[...]).astype(LOW)
        for j in range(count // 2):
            for target, core in ((own, place[0]), (other, 1 - place[0])):
                start = pl.multiple_of(j * rows + core * half, 16)
                target[j, :half, :] = whole[pl.ds(start, half), :HALF]
                target[j, half:, :] = whole[pl.ds(start, half), HALF:]

    return kernel_call(
        body,
        [((count // 2, rows, HALF), LOW)] * 2,
        (place, context, branch),
        [pltpu.VMEM((HALF, D), LOW)],
    )


def out_weight(place, count, own, got):
    rows = D // count
    half = rows // 2
    if half % 16:
        first = place[0] == 0
        own, got = [p.reshape(count // 2, 2, half, HALF) for p in (own, got)]
        both = jnp.stack([jnp.where(first, own, got), jnp.where(first, got, own)], axis=1)
        return both.transpose(0, 1, 3, 2, 4).reshape(HALF, D)

    def body(place, own, got, whole):
        for i in range(count // 2):
            j = ((((place[1] >> 1) & 1) ^ (i >> 1)) << 1) | (i & 1)
            for source, core in ((own, place[0]), (got, 1 - place[0])):
                start = pl.multiple_of(j * rows + core * half, 16)
                whole[pl.ds(start, half), :HALF] = source[i, :half, :]
                whole[pl.ds(start, half), HALF:] = source[i, half:, :]

    return kernel_call(body, [((HALF, D), LOW)], (place, own, got))[0]


def attend_weights_grad(place, count, hidden, change, out_own, out_got, bits, sums=None):
    rows = D // count
    extra = 0 if sums is None else 16

    def vec_rows(sums):
        attend, feed = [
            jnp.concatenate([part[...][:8] for part in pair], axis=0) for pair in (sums[::2], sums[1::2])
        ]
        row = lax.broadcasted_iota(jnp.int32, (16, 1), 0) % 8
        down = jnp.concatenate(
            [jnp.broadcast_to(part[...][6:7], (8, D)) for part in sums[1::2]], axis=0
        )
        return jnp.concatenate([jnp.where(row == 3, down, attend), feed], axis=1).astype(LOW)

    if (rows // 2) % 16:
        first = place[0] == 0
        out_parts = jnp.concatenate(
            [jnp.where(first, out_own, out_got), jnp.where(first, out_got, out_own)]
        )
        parts = mm_rows(hidden, change).astype(LOW).reshape(count, rows, 3 * HALF)
        whole = jnp.concatenate([parts, out_parts], axis=2).reshape(D, WIDTH)
        return whole if sums is None else (whole, vec_rows(sums))

    def body(place, hidden, change, out_own, out_got, *rest):
        *sums, kept, sent, whole = rest
        for i in range(3):
            cols = slice(i * HALF, (i + 1) * HALF)
            whole[:, cols] = mm_rows(hidden[...], change[:, cols]).astype(LOW)
        for source, core in ((out_own, place[0]), (out_got, 1 - place[0])):
            for j in range(count // 2):
                start = pl.multiple_of((core * (count // 2) + j) * rows, 16)
                whole[pl.ds(start, rows), 3 * HALF :] = source[j]
        spread_rows(place, bits, whole, kept, sent)
        if sums:
            sent[D // 2 :, :] = vec_rows(sums)

    return kernel_call(
        body,
        [((D // 2, WIDTH), LOW), ((D // 2 + extra, WIDTH), LOW)],
        (place, hidden, change, out_own, out_got) + tuple(sums or ()),
        [pltpu.VMEM((D, WIDTH), LOW)],
    )


class Links:
    def __init__(self):
        self.count = lax.axis_size("dp")
        self.bits = self.count.bit_length() - 1
        self.dp = lax.axis_index("dp")
        self.x = lax.axis_index("x")
        self.c = lax.axis_index("c")
        self.plain = (D // self.count // 2) % 16 != 0

    def own(self, bit):
        if bit == "c":
            return self.c
        if bit == "x":
            return self.x
        return (self.dp >> bit) & 1

    def flip(self, value, bit):
        step = {"c": 1, "x": 2}.get(bit)
        if step is None:
            step = 4 << bit
        pairs = [(place, place ^ step) for place in range(4 * self.count)]
        return lax.ppermute(value, AXES, pairs)

    def order(self, names):
        bits = {"x": ["x"], "y": [0], "1": [1], "2": list(range(self.bits))[:1:-1]}
        return [bit for name in names for bit in bits[name]]

class Gather:
    def __init__(self, links, shard, names):
        self.links, self.shape = links, shard.shape
        self.bits = links.order(names)
        self.held = shard.reshape((1,) * len(self.bits) + shard.shape)
        self.got = None
        self.layers = [None, None]

    def axis(self, bit):
        return 0 if bit == "x" else self.links.bits - bit

    def joined(self, held, got, bit):
        first = self.links.own(bit) == 0
        return jnp.concatenate(
            [jnp.where(first, held, got), jnp.where(first, got, held)], axis=self.axis(bit)
        )

    def send(self):
        bit = self.bits[0]
        if len(self.bits) > 1 or bit == "x":
            self.got = self.links.flip(self.held, bit)
        else:
            first = self.links.flip(self.held[:1], bit)
            self.got = [first, self.links.flip(tie(self.held[1:], first), bit)]

    def join(self):
        held = self.held
        self.held = self.joined(held, self.got, self.bits[0])
        self.bits = self.bits[1:]

    def whole(self, layer):
        if self.bits[0] == "x":
            whole = jnp.where(self.links.x == layer, self.held, self.got)
        else:
            whole = self.joined(self.held[layer : layer + 1], self.got[layer], self.bits[0])
        return whole.reshape((self.links.count,) + self.shape)

    def pieces(self, layer):
        if self.bits[0] == "x":
            return [part.reshape((-1,) + self.shape) for part in (self.held, self.got)]
        return [
            part.reshape((-1,) + self.shape) for part in (self.held[layer : layer + 1], self.got[layer])
        ]

    def weight(self, layer, rows, lanes):
        if self.links.plain:
            return self.whole(layer).reshape(rows, lanes)
        bit, size = self.bits[0], self.shape[0]

        def copies(place, refs):
            if bit == "x":
                own = place[2] == layer
                for source, condition in zip(refs, (own, jnp.logical_not(own))):
                    for chip in range(source.shape[0]):
                        yield source.at[chip], chip * size, condition
            else:
                for side, source in enumerate(refs):
                    one = ((place[1] >> bit) & 1) ^ side
                    for i in range(source.shape[0]):
                        chip = ((i >> bit) << (bit + 1)) | (one << bit) | (i & ((1 << bit) - 1))
                        yield source.at[i], chip * size, None

        return Weight((rows, lanes), self.pieces(layer), copies)


class Spread:
    def __init__(self, links, value, names):
        self.links, self.held = links, value
        self.bits = links.order(names)

    def send(self):
        self.got = self.links.flip(self.held, self.bits[0])

    def join(self):
        held, got = self.held, self.got
        if self.bits[0] == "x":
            first = self.links.x == 0
            self.held = jnp.concatenate([jnp.where(first, held, got), jnp.where(first, got, held)])
        else:
            self.held = (held.astype(WIDE) + got.astype(WIDE)).astype(LOW)
        self.bits = self.bits[1:]


class Scatter:
    def __init__(self, links, parts, names, extra=None, pieces=()):
        self.links, self.bits = links, links.order(names)
        self.pieces = list(pieces) + [1] * len(self.bits)
        self.plain = links.plain
        self.extra = extra
        if self.plain:
            self.kept = parts
        else:
            self.kept, self.sent = parts
            if extra is not None:
                self.extra = self.sent[self.kept.shape[0] :]

    def send(self):
        if not self.plain:
            number = self.pieces.pop(0)
            size = self.kept.shape[0] // number
            cuts = [i * size for i in range(number)] + [self.sent.shape[0]]
            self.got = tuple(
                self.links.flip(self.sent[a:b], self.bits[0]) for a, b in zip(cuts, cuts[1:])
            )

    def add(self, token, after=()):
        if self.plain:
            if self.bits:
                self.add_plain(tie(self.kept, token))
            return self.kept
        kept = tie(self.kept, token)
        self.kept, self.sent, self.extra = add_rows(kept, self.got, self.extra, len(self.bits) == 1, after)
        self.bits = self.bits[1:]
        return self.kept

    def add_plain(self, parts):
        links, lanes = self.links, parts.shape[1]
        has_x = "x" in self.bits
        held = parts.reshape((2,) * (links.bits + has_x) + (-1, lanes))
        for bit in self.bits:
            own, axis = links.own(bit), links.bits if bit == "x" else links.bits - 1 - bit
            kept = lax.dynamic_slice_in_dim(held, own, 1, axis)
            sent = lax.dynamic_slice_in_dim(held, 1 - own, 1, axis)
            if self.extra is None:
                got = links.flip(sent, bit)
            else:
                got = links.flip(jnp.concatenate([sent.reshape(-1, lanes), self.extra]), bit)
                split = got.shape[0] - self.extra.shape[0]
                self.extra = (self.extra.astype(WIDE) + got[split:].astype(WIDE)).astype(LOW)
                got = got[:split].reshape(sent.shape)
            held = (kept.astype(WIDE) + got.astype(WIDE)).astype(LOW)
        self.kept, self.bits = held.reshape(-1, lanes), []


class Pair:
    def __init__(self, w, u):
        self.w, self.u = w, u

    def merge(self, token, after=()):
        w, u = self.w, self.u
        if w.plain:
            half = u.add(w.add(token)).shape[0]
            self.kept = jnp.concatenate(
                [u.kept, jnp.concatenate([w.kept[:half], w.kept[half:]], axis=1)]
            )
            return self.kept
        half = u.kept.shape[0] // 2

        def body(place, w_kept, w_got, u_kept, u_got, kept, sent):
            for at, target in ((0, kept), (half, sent)):
                rows = slice(at, at + half)
                target[:half, :] = (
                    u_kept[rows, :].astype(WIDE) + u_got[rows, :].astype(WIDE)
                ).astype(LOW)
                for i in range(2):
                    rows = slice(2 * at + i * half, 2 * at + (i + 1) * half)
                    target[half:, i * D : (i + 1) * D] = (
                        w_kept[rows, :].astype(WIDE) + w_got[rows, :].astype(WIDE)
                    ).astype(LOW)

        self.kept, sent = kernel_call(
            body,
            [((2 * half, WIDTH), LOW)] * 2,
            (jnp.zeros((1,), jnp.int32), tie(w.kept, token), w.got[0], u.kept, u.got[0]),
            after=after,
        )
        self.got = w.links.flip(sent, w.bits[1])
        return self.kept

    def finish(self, token, after=()):
        if self.w.plain:
            return self.kept

        def body(place, kept, got, out):
            out[...] = (kept[...].astype(WIDE) + got[...].astype(WIDE)).astype(LOW)

        self.kept = kernel_call(
            body,
            [(self.kept.shape, LOW)],
            (jnp.zeros((1,), jnp.int32), tie(self.kept, token), self.got),
            after=after,
        )[0]
        return self.kept


def tie(value, token):
    return lax.optimization_barrier((value, token))[0]


def add_rows(kept, got, extra, last, after):
    rows, lanes = kept.shape
    more = 0 if extra is None else extra.shape[0]
    half = rows if last else rows // 2

    def body(place, kept, got, *rest):
        size = rows // len(got)
        if more:
            extra_sum = (rest[0][...].astype(WIDE) + got[-1][size:, :].astype(WIDE)).astype(LOW)
            rest[-1][...] = extra_sum
            rest = rest[1:-1]
            if not last:
                rest[1][half:, :] = extra_sum
        step = min(size, half)
        for at in range(0, rows, step):
            piece = got[at // size]
            start = at % size
            total = (
                kept[at : at + step, :].astype(WIDE) + piece[start : start + step, :].astype(WIDE)
            ).astype(LOW)
            target, to = (rest[0], at) if at < half else (rest[1], at - half)
            target[to : to + step, :] = total

    outs = [((half, lanes), LOW)]
    if not last:
        outs.append(((half + more, lanes), LOW))
    if more:
        outs.append(((more, lanes), LOW))
    ins = (jnp.zeros((1,), jnp.int32), kept, got) + ((extra,) if more else ())
    results = list(kernel_call(body, outs, ins, after=after))
    extra = results.pop() if more else None
    return results[0], None if last else results[1], extra


def adam_update(master, first, second, gradient):
    first_new = BETA_ONE * first + (1.0 - BETA_ONE) * gradient
    second_new = BETA_TWO * second + (1.0 - BETA_TWO) * gradient * gradient
    update = first_new / BIAS_ONE / (jnp.sqrt(second_new / BIAS_TWO) + ADAM_EPSILON)
    return (update + WEIGHT_DECAY * master, first_new, second_new)


def on_device(
    inputs,
    cotangent,
    in_master,
    in_first,
    in_second,
    down_master,
    down_first,
    down_second,
    vec_master,
    vec_first,
    vec_second,
):
    links = Links()
    count, x, c = links.count, links.x, links.c
    rows = D // count
    half_rows = rows // 2
    vec_part = VEC // count
    first_core = c == 0
    first_chip = x == 0
    place = jnp.stack([c, links.dp, x]).astype(jnp.int32)

    def mine(one, other):
        return jnp.where(first_core, one, other)

    def trade(part):
        return links.flip(part, "c")

    def trade_blocks(part):
        return tuple(trade(part[i : i + BLOCK]) for i in range(0, SEQ, BLOCK))

    in_low = in_master[0].astype(LOW)
    out_rows = in_low[:, 3 * D :]
    pieces = []
    for core in (0, 1):
        out_half = out_rows[core * half_rows : (core + 1) * half_rows]
        pieces.append(
            jnp.concatenate(
                [in_low[:, i * D + core * HALF : i * D + (core + 1) * HALF] for i in range(3)]
                + [jnp.concatenate([out_half[:, :HALF], out_half[:, HALF:]], axis=0)],
                axis=1,
            )
        )
    got = trade(mine(pieces[1], in_low[:, :WIDTH]))
    attend_shard = mine(pieces[0], got)
    up_shard = mine(got, in_low[:, WIDTH:])
    down_shard = down_master[0].astype(LOW)

    placed = lax.dynamic_update_slice(
        jnp.zeros((VEC,), WIDE), vec_master[0], (links.dp * vec_part,)
    ).reshape(-1, D)
    high = lax.reduce_precision(placed, 8, 7)
    vec_both = jnp.pad(jnp.concatenate([high, placed - high]).astype(LOW), ((0, 4), (0, 0)))
    vec_got = trade(vec_both)
    vec_both = jnp.concatenate([mine(vec_both, vec_got), mine(vec_got, vec_both)])

    small = Spread(links, vec_both, "yx21")
    attend_in = Gather(links, attend_shard, "2xy1")
    down_in = Gather(links, down_shard, "2y1x")
    up_in = Gather(links, up_shard, "12xy")
    streams = {"v": small, "t": attend_in, "w": down_in, "u": up_in}
    for name in "twu":
        streams[name].send()
    small.held = tie(small.held, attend_in.got)
    small.send()
    turns = "tvwuvtwuvtwvu" if links.bits == 3 else "twuv" * links.bits + "v"
    for name in turns:
        streams[name].join()
        if streams[name].bits:
            streams[name].send()
    vectors = small.held.reshape(2, 32, D)
    vecs = []
    for layer in (0, 1):
        vec = vectors[layer].astype(WIDE)
        vecs.append([vec[i : i + 6] + vec[i + 6 : i + 12] for i in (0, 16)])

    def attend_weights(layer):
        if links.plain:
            parts = attend_in.whole(layer)[None]
        else:
            parts = jnp.stack(attend_in.pieces(layer))
        parts = parts[..., 3 * HALF :].reshape(parts.shape[0], 2, -1, rows, HALF)
        own = mine(parts[:, 0], parts[:, 1]).reshape(-1, rows, HALF)
        got = trade(mine(parts[:, 1], parts[:, 0]).reshape(-1, rows, HALF))
        return attend_in.weight(layer, D, WIDTH), out_weight(place, count, own, got)

    qkv, out, up, down = [None] * 2, [None] * 2, [None] * 2, [None] * 2
    qkv[0], out[0] = attend_weights(0)
    hidden = [lax.dynamic_slice_in_dim(inputs, x * SEQ, SEQ, 0)]
    part, mixing_0, chances_0, context_0 = attend_first(
        place, hidden[0], qkv[0], out[0], vecs[0][0]
    )
    up[0] = up_in.weight(0, D, WIDTH)
    down[0] = down_in.weight(0, WIDTH, D)
    next_hidden, normed_0, spread_0, part, active_0, slope_0 = feed_forward(
        place, hidden[0], part, trade_blocks(part), vecs[0][0], vecs[0][1], up[0], down[0]
    )
    hidden.append(next_hidden)
    qkv[1], out[1] = attend_weights(1)
    next_hidden, normed_1, spread_1, part, mixing_1, chances_1, context_1 = attend_next(
        place, hidden[1], part, trade_blocks(part), vecs[0][1], vecs[0][0], qkv[1], out[1], vecs[1][0]
    )
    hidden.append(next_hidden)
    up[1] = up_in.weight(1, D, WIDTH)
    down[1] = down_in.weight(1, WIDTH, D)
    next_hidden, normed_2, spread_2, part, active_1, slope_1 = feed_forward(
        place, hidden[2], part, trade_blocks(part), vecs[1][0], vecs[1][1], up[1], down[1]
    )
    hidden.append(next_hidden)

    class Sections:
        def __init__(self, values):
            low, high = mine(values[0], values[1]), mine(values[2], values[3])
            self.own = jnp.where(first_chip, low, high)
            self.away = jnp.where(first_chip, high, low)

        def send(self, token):
            self.got = links.flip(tie(self.away, token), "x")

        def whole(self):
            return jnp.concatenate(
                [jnp.where(first_chip, self.own, self.got), jnp.where(first_chip, self.got, self.own)]
            )[None]

    def home(one, other):
        got = links.flip(jnp.where(first_chip, other, one), "x")
        own = jnp.where(first_chip, one, other)
        return jnp.where(first_chip, own, got), jnp.where(first_chip, got, own)

    names = {"w": "x1y2", "u": "1xy2", "t": "y21", "T": "y12", "W": "xy12", "U": "1xy2"}
    bits = {name: links.order(order) for name, order in names.items()}

    def feed_sums(layer, active, branch, hidden, change):
        both = "wu" if layer else "WU"
        parts = feed_weights_grad(
            place, active, branch, hidden, change, bits[both[0]], bits[both[1]]
        )
        sums = [Scatter(links, part, names[name]) for part, name in zip(parts, both)]
        for each in sums:
            each.send()
        return sums

    def attend_sums(layer, context, branch, hidden, change, vector_sums=None):
        own = "t" if vector_sums is None else "T"
        out_own, out_other = out_weight_grad(place, count, context, branch)
        parts = attend_weights_grad(
            place, count, hidden, change, out_own, trade(out_other), bits[own], vector_sums
        )
        extra = None
        if vector_sums is not None:
            parts, extra = parts if links.plain else (parts, True)
        total = Scatter(links, parts, names[own], extra)
        total.send()
        return total

    cotangent_rows = lax.dynamic_slice_in_dim(cotangent, x * SEQ, SEQ, 0)
    last, summed, branch, change, part, feed_vec_1 = feed_last(
        place, hidden[3], part, trade_blocks(part), vecs[1][0], vecs[1][1], up[1], down[1], slope_1, cotangent_rows
    )
    part_got = trade_blocks(part)
    outputs = Sections(hidden[1:] + [last])
    w_1, u_1 = feed_sums(1, active_1, branch, hidden[3], change)
    grad_3, summed, branch, change, part, attend_vec_1 = attend_back(
        place, tie(summed, u_1.kept), part, part_got, normed_2, spread_2, vecs[1][0], qkv[1], out[1], mixing_1, chances_1
    )
    part_got = trade_blocks(part)
    t_1 = attend_sums(1, context_1, branch, hidden[2], change)
    grad_2, summed, branch, change, part, feed_vec_0 = feed_back(
        place, tie(summed, t_1.kept), part, part_got, normed_1, spread_1, vecs[0][1], up[0], down[0], slope_0
    )
    part_got = trade_blocks(part)
    token = w_1.add(branch)
    w_1.send()
    token = u_1.add(token)
    u_1.send()
    w_0, u_0 = feed_sums(0, active_0, tie(branch, token), hidden[1], change)
    outputs.send(t_1.kept)
    token = u_0.kept
    grad_1, summed, branch, change, part, attend_vec_0 = attend_back(
        place, tie(summed, token), part, part_got, normed_0, spread_0, vecs[0][0], qkv[0], out[0], mixing_0, chances_0, (outputs.got,)
    )
    part_got = trade_blocks(part)
    token = t_1.add(grad_1)
    t_1.send()
    token = w_1.add(token)
    w_1.send()
    token = u_1.add(token)
    u_1.send()
    t_0 = attend_sums(
        0,
        context_0,
        tie(branch, token),
        hidden[0],
        change,
        (attend_vec_0, feed_vec_0, attend_vec_1, feed_vec_1),
    )
    grad_0 = (summed + part.astype(WIDE) + jnp.concatenate(part_got).astype(WIDE)).astype(LOW)
    grads = Sections([grad_0, grad_1, grad_2, grad_3])
    token = t_0.kept
    sums = {"w": w_1, "u": u_1, "t": t_1, "W": w_0, "U": u_0, "T": t_0}
    pairs = {"p": Pair(w_1, u_1), "P": Pair(w_0, u_0)}
    pairs["q"], pairs["Q"] = pairs["p"], pairs["P"]
    after = ()
    for name in ORDER:
        if name == "o":
            outputs.send(token)
        elif name == "g":
            grads.send(token)
        elif name in "OG":
            after = (outputs.got,) if name == "O" else (grads.got,)
        elif name in "pP":
            token, after = pairs[name].merge(token, after), ()
        elif name in "qQ":
            token, after = pairs[name].finish(token, after), ()
        else:
            token = sums[name].add(token, after)
            after = ()
            if sums[name].bits:
                sums[name].send()
            elif name == "T":
                sent = jnp.concatenate([jnp.where(first_chip, t_1.kept, t_0.kept), t_0.extra])
                last_got = links.flip(sent, "x")
    ours, other = home(pairs["P"].kept, pairs["p"].kept)
    up_sum = jnp.concatenate([ours[:half_rows], other[:half_rows]])
    down_sum = jnp.concatenate(
        [part[half_rows:, at : at + D] for part in (ours, other) for at in (0, D)]
    )

    got = last_got
    attend_sum = jnp.where(first_chip, t_0.kept, t_1.kept).astype(WIDE) + got[:rows].astype(WIDE)
    attend_sum = attend_sum.astype(LOW)
    vec_total = (t_0.extra.astype(WIDE) + got[rows:].astype(WIDE)).astype(LOW)
    section_outputs, section_input_grads = outputs.whole(), grads.whole()

    got = trade(jnp.concatenate([mine(up_sum, attend_sum), vec_total]))
    vec_total = vec_total.astype(WIDE) + got[rows:].astype(WIDE)
    got = got[:rows]
    kept = mine(attend_sum, up_sum)
    first, second = mine(kept, got), mine(got, kept)

    def joined(one, other):
        out_one, out_other = one[:, 3 * HALF :], other[:, 3 * HALF :]
        out_cols = [
            jnp.concatenate([out_one[i : i + half_rows], out_other[i : i + half_rows]])
            for i in (0, half_rows)
        ]
        cols = [part[:, i * HALF : (i + 1) * HALF] for i in range(3) for part in (one, other)]
        return jnp.concatenate(cols + out_cols, axis=1)

    in_sum = mine(joined(first, second), jnp.concatenate([first, second], axis=1))
    in_sum = in_sum.astype(WIDE)[None]
    down_sum = down_sum.astype(WIDE)[None]
    vec_sum = lax.dynamic_slice(vec_total, (8 * x, D * c), (6, D)).reshape(VEC)
    vec_sum = lax.dynamic_slice(vec_sum, (links.dp * vec_part,), (vec_part,))[None]

    in_step, in_first_new, in_second_new = adam_update(in_master, in_first, in_second, in_sum)
    down_step, down_first_new, down_second_new = adam_update(
        down_master, down_first, down_second, down_sum
    )
    vec_step, vec_first_new, vec_second_new = adam_update(
        vec_master, vec_first, vec_second, vec_sum
    )
    return (
        section_outputs,
        section_input_grads,
        in_sum,
        down_sum,
        vec_sum,
        in_step,
        in_first_new,
        in_second_new,
        down_step,
        down_first_new,
        down_second_new,
        vec_step,
        vec_first_new,
        vec_second_new,
    )


def solution(mesh):
    grid = Mesh(mesh.devices.reshape(mesh.shape["dp"], 2, 2), AXES)
    tokens = P("dp", None)
    matrix = P(("x", "c"), "dp", None)
    vector = P(("x", "c"), "dp")
    return jax.shard_map(
        on_device,
        mesh=grid,
        in_specs=(tokens,) * 2 + (matrix,) * 6 + (vector,) * 3,
        out_specs=(matrix,) * 4 + (vector,) + (matrix,) * 6 + (vector,) * 3,
        check_vma=False,
    )
```

```python
import jax
import jax.numpy as jnp
from jax import lax
from jax.experimental import pallas as pl
from jax.experimental.pallas import tpu as pltpu
from jax.sharding import Mesh
from jax.sharding import PartitionSpec as P

D = 768
HEADS = 12
HEAD_DIM = 64
FF = 3072
SEQ = 512
VEC = 4608
HALF = D // 2
WIDTH = FF // 2
BLOCK = 128
STEP = 256
PAIR = 2 * HEAD_DIM
VMEM_LIMIT = 14 * 2**20
FLOPS = 10**8
ORDER = "UWTtpgTUWtTPGqQ"

NORM_EPSILON = 1e-05
BETA_ONE = 0.9
BETA_TWO = 0.98
BIAS_ONE = 1.0 - 0.9**10
BIAS_TWO = 1.0 - 0.98**10
WEIGHT_DECAY = 0.01
ADAM_EPSILON = 1e-06
ROOT_HALF = 0.7071067811865476
ROOT_TWO_PI = 2.5066282746310002
SCALE = HEAD_DIM**-0.5

AXES = ("dp", "x", "c")
LOW = jnp.bfloat16
WIDE = jnp.float32


def mm(a, b):
    return lax.dot_general(a, b, (((1,), (0,)), ((), ())), preferred_element_type=WIDE)
def mm_cols(a, b):
    return lax.dot_general(a, b, (((1,), (1,)), ((), ())), preferred_element_type=WIDE)
def mm_rows(a, b):
    return lax.dot_general(a, b, (((0,), (0,)), ((), ())), preferred_element_type=WIDE)

class Weight:
    def __init__(self, shape, pieces, copies):
        self.shape, self.pieces, self.copies = shape, pieces, copies


class Arriving:
    def __init__(self, place, weight, refs, scratch, sem):
        self.scratch, self.sem, self.waiting = scratch, sem, True
        for source, row, condition in weight.copies(place, refs):
            copy = pltpu.make_async_copy(
                source, scratch.at[pl.ds(pl.multiple_of(row, 16), source.shape[0])], sem
            )
            if condition is None:
                copy.start()
            else:
                pl.when(condition)(copy.start)

    def __getitem__(self, at):
        if self.waiting:
            pltpu.make_async_copy(self.scratch, self.scratch, self.sem).wait()
            self.waiting = False
        return self.scratch[at]


def kernel_call(body, outs, ins, scratch=(), after=()):
    scratch = list(scratch)
    own_scratch = len(scratch)
    specs, flat = [], []
    for part in ins:
        if isinstance(part, Weight):
            specs += [pl.BlockSpec(memory_space=pl.ANY)] * len(part.pieces)
            flat += part.pieces
            scratch += [pltpu.VMEM(part.shape, LOW), pltpu.SemaphoreType.DMA]
        else:
            group = part if isinstance(part, tuple) else (part,)
            space = pltpu.VMEM if flat else pltpu.SMEM
            specs += [pl.BlockSpec(memory_space=space)] * len(group)
            flat += group

    specs += [pl.BlockSpec(memory_space=pl.ANY)] * len(after)
    flat += after

    def whole_body(*refs):
        at = [0]

        def take(number):
            at[0] += number
            return list(refs[at[0] - number : at[0]])

        inputs = [
            take(len(part.pieces) if isinstance(part, Weight) else len(part))
            if isinstance(part, (Weight, tuple))
            else take(1)[0]
            for part in ins
        ]
        take(len(after))
        results = take(len(outs) + own_scratch)
        for i, part in enumerate(ins):
            if isinstance(part, Weight):
                inputs[i] = Arriving(inputs[0], part, inputs[i], *take(2))
        body(*inputs, *results)

    return pl.pallas_call(
        whole_body,
        out_shape=[jax.ShapeDtypeStruct(s, d) for s, d in outs],
        in_specs=specs,
        out_specs=[pl.BlockSpec(memory_space=pltpu.VMEM)] * len(outs),
        scratch_shapes=scratch,
        compiler_params=pltpu.CompilerParams(vmem_limit_bytes=VMEM_LIMIT),
        cost_estimate=pl.CostEstimate(flops=FLOPS, bytes_accessed=1000, transcendentals=0),
    )(*flat)


def norm_rows(total, vec, normed_ref, spread_ref, out_ref, rows):
    mean = jnp.mean(total, axis=-1, keepdims=True)
    centered = total - mean
    spread = lax.rsqrt(jnp.mean(centered * centered, axis=-1, keepdims=True) + NORM_EPSILON)
    normed = centered * spread
    normed_ref[rows, :] = normed.astype(LOW)
    spread_ref[rows, :] = spread
    out_ref[rows, :] = (normed * vec[4:5, :] + vec[5:6, :]).astype(LOW)

def joined_norm(before, own, got, bias, vec, normed, spread, out):
    for i in range(SEQ // BLOCK):
        rows = slice(i * BLOCK, (i + 1) * BLOCK)
        total = before[rows, :].astype(WIDE) + own[rows, :].astype(WIDE) + got[i][...].astype(WIDE) + bias
        norm_rows(total, vec, normed, spread, out, rows)

def half_row(place, row):
    return jnp.where(place[0] == 0, row[:, :HALF], row[:, HALF:])

NORM_OUTS = [((SEQ, D), LOW), ((SEQ, D), LOW), ((SEQ, 1), WIDE)]

def attend_body(place, hidden, w_qkv, w_out, vec, part, mixing, chances, context):
    bias = jnp.concatenate([half_row(place, vec[0:1, :]), jnp.zeros((1, HALF), WIDE), half_row(place, vec[1:2, :])], axis=1)
    for i in range(3):
        cols = slice(i * HALF, (i + 1) * HALF)
        mixing[:, cols] = (mm(hidden[...], w_qkv[:, cols]) + bias[:, cols]).astype(LOW)
    lane = lax.broadcasted_iota(jnp.int32, (SEQ, PAIR), 1)
    first = lane < HEAD_DIM
    for pair in range(HEADS // 4):
        at = pair * PAIR
        queries = mixing[:, at : at + PAIR] * jnp.asarray(SCALE, LOW)
        keys = mixing[:, HALF + at : HALF + at + PAIR]
        values = mixing[:, 2 * HALF + at : 2 * HALF + at + PAIR]
        sums = []
        for side in range(2):
            mine = first if side == 0 else ~first
            scores = mm_cols(jnp.where(mine, queries, jnp.zeros_like(queries)), keys)
            scores = jnp.exp(scores - jnp.max(scores, axis=-1, keepdims=True))
            low = (scores * (1.0 / jnp.sum(scores, axis=-1, keepdims=True))).astype(LOW)
            chances[2 * pair + side] = low
            sums.append(mm(low, values))
        context[:, at : at + PAIR] = jnp.where(first, sums[0], sums[1]).astype(LOW)
    for i in range(2):
        cols = slice(i * HALF, (i + 1) * HALF)
        part[:, cols] = mm(context[...], w_out[:, cols]).astype(LOW)

ATTEND_OUTS = [((SEQ, D), LOW), ((SEQ, 3 * HALF), LOW), ((HEADS // 2, SEQ, SEQ), LOW), ((SEQ, HALF), LOW)]

def attend_first(place, hidden, w_qkv, w_out, vec):
    return kernel_call(attend_body, ATTEND_OUTS, (place, hidden, w_qkv, w_out, vec))

def attend_next_body(place, before, own, got, feed_vec, last_vec, w_qkv, w_out, vec, hidden, normed, spread, *rest):
    joined_norm(before, own, got, last_vec[3:4, :], feed_vec, normed, spread, hidden)
    attend_body(place, hidden, w_qkv, w_out, vec, *rest)

def attend_next(place, before, own, got, feed_vec, last_vec, w_qkv, w_out, vec):
    return kernel_call(attend_next_body, NORM_OUTS + ATTEND_OUTS, (place, before, own, got, feed_vec, last_vec, w_qkv, w_out, vec))

def feed_body(place, before, own, got, vec, feed_vec, w_up, w_down, hidden, normed, spread, part, active, slope):
    joined_norm(before, own, got, vec[2:3, :], vec, normed, spread, hidden)
    for i in range(WIDTH // STEP):
        cols = slice(i * STEP, (i + 1) * STEP)
        row, col = divmod(i * STEP, D)
        bias = jnp.where(place[0] == 0, feed_vec[row : row + 1, col : col + STEP], feed_vec[row + 2 : row + 3, col : col + STEP])
        for j in range(2):
            rows = slice(j * SEQ // 2, (j + 1) * SEQ // 2)
            value = mm(hidden[rows, :], w_up[:, cols]) + bias
            curve = 0.5 * (1.0 + lax.erf(value * ROOT_HALF))
            active[rows, cols] = (value * curve).astype(LOW)
            slope[rows, cols] = (curve + value * jnp.exp(-0.5 * value * value) * (1.0 / ROOT_TWO_PI)).astype(LOW)
    for i in range(2):
        cols = slice(i * HALF, (i + 1) * HALF)
        part[:, cols] = mm(active[...], w_down[:, cols]).astype(LOW)

FEED_OUTS = NORM_OUTS + [((SEQ, D), LOW), ((SEQ, WIDTH), LOW), ((SEQ, WIDTH), LOW)]
def feed_forward(place, before, own, got, vec, feed_vec, w_up, w_down):
    return kernel_call(feed_body, FEED_OUTS, (place, before, own, got, vec, feed_vec, w_up, w_down))

def norm_backward(grad_rows, normed, spread, vec, summed, branch, sums, bias_row):
    totals = [jnp.zeros((1, D), WIDE)] * 3
    for i in range(SEQ // BLOCK):
        rows = slice(i * BLOCK, (i + 1) * BLOCK)
        grad = grad_rows(i, rows)
        n = normed[rows, :].astype(WIDE)
        through = grad * vec[4:5, :]
        out = spread[rows, :] * (
            through
            - jnp.mean(through, axis=-1, keepdims=True)
            - n * jnp.mean(through * n, axis=-1, keepdims=True)
        )
        summed[rows, :] = out
        branch[rows, :] = out.astype(LOW)
        terms = (out, grad * n, grad)
        totals = [t + jnp.sum(term, axis=0, keepdims=True) for t, term in zip(totals, terms)]
    return totals


def feed_back_core(place, grad_rows, normed, spread, feed_vec, w_up, w_down, slope, summed, branch, change, part, sums):
    once = jnp.where(place[0] == 0, 1.0, 0.0)
    branch_sum, gain_sum, bias_sum = norm_backward(grad_rows, normed, spread, feed_vec, summed, branch, sums, 0)
    sums[...] = jnp.zeros_like(sums)
    sums[4:5, :] = gain_sum * once
    sums[5:6, :] = bias_sum * once
    sums[6:7, :] = branch_sum * once
    for i in range(WIDTH // STEP):
        cols = slice(i * STEP, (i + 1) * STEP)
        row, col = divmod(i * STEP, D)
        total = jnp.zeros((1, STEP), WIDE)
        for j in range(2):
            rows = slice(j * SEQ // 2, (j + 1) * SEQ // 2)
            value = (mm_cols(branch[rows, :], w_down[cols, :]) * slope[rows, cols].astype(WIDE)).astype(LOW)
            change[rows, cols] = value
            total = total + jnp.sum(value.astype(WIDE), axis=0, keepdims=True)
        sums[row : row + 1, col : col + STEP] = total * once
        sums[row + 2 : row + 3, col : col + STEP] = total * (1.0 - once)
    for i in range(2):
        rows = slice(i * HALF, (i + 1) * HALF)
        part[:, rows] = mm_cols(change[...], w_up[rows, :]).astype(LOW)

BACK_OUTS = [((SEQ, D), WIDE), ((SEQ, D), LOW)]

def feed_last_body(place, before, own, got, last_vec, feed_vec, w_up, w_down, slope, cot, out, summed, branch, change, part, sums, normed, spread):
    joined_norm(before, own, got, last_vec[3:4, :], feed_vec, normed, spread, out)
    feed_back_core(place, lambda i, rows: cot[rows, :].astype(WIDE), normed, spread, feed_vec, w_up, w_down, slope, summed, branch, change, part, sums)

def feed_last(place, before, own, got, last_vec, feed_vec, w_up, w_down, slope, cot):
    return kernel_call(feed_last_body,
        [((SEQ, D), LOW)] + BACK_OUTS + [((SEQ, WIDTH), LOW), ((SEQ, D), LOW), ((8, D), WIDE)],
        (place, before, own, got, last_vec, feed_vec, w_up, w_down, slope, cot),
        [pltpu.VMEM((SEQ, D), LOW), pltpu.VMEM((SEQ, 1), WIDE)])

def joined_grad(before, own, got, grad):
    def rows_of(i, rows):
        value = (before[rows, :] + own[rows, :].astype(WIDE) + got[i][...].astype(WIDE)).astype(LOW)
        grad[rows, :] = value
        return value.astype(WIDE)
    return rows_of

def feed_back_body(place, before, own, got, normed, spread, feed_vec, w_up, w_down, slope, grad, summed, branch, change, part, sums):
    feed_back_core(place, joined_grad(before, own, got, grad), normed, spread, feed_vec, w_up, w_down, slope, summed, branch, change, part, sums)

def feed_back(place, before, own, got, normed, spread, feed_vec, w_up, w_down, slope):
    return kernel_call(feed_back_body,
        [((SEQ, D), LOW)] + BACK_OUTS + [((SEQ, WIDTH), LOW), ((SEQ, D), LOW), ((8, D), WIDE)],
        (place, before, own, got, normed, spread, feed_vec, w_up, w_down, slope))

def attend_back_body(place, before, own, got, normed, spread, vec, w_qkv, w_out, mixing, chances, grad, summed, branch, change, part, sums, context_grad):
    once = jnp.where(place[0] == 0, 1.0, 0.0)
    branch_sum, gain_sum, bias_sum = norm_backward(joined_grad(before, own, got, grad), normed, spread, vec, summed, branch, sums, 2)
    sums[...] = jnp.zeros_like(sums)
    sums[2:3, :] = branch_sum * once
    sums[4:5, :] = gain_sum * once
    sums[5:6, :] = bias_sum * once
    context_grad[...] = mm_cols(branch[...], w_out[...]).astype(LOW)
    first = lax.broadcasted_iota(jnp.int32, (SEQ, PAIR), 1) < HEAD_DIM
    for pair in range(HEADS // 4):
        at = pair * PAIR
        queries = mixing[:, at : at + PAIR]
        keys = mixing[:, HALF + at : HALF + at + PAIR]
        values = mixing[:, 2 * HALF + at : 2 * HALF + at + PAIR]
        outer = context_grad[:, at : at + PAIR]
        parts = []
        for side in range(2):
            mine = first if side == 0 else ~first
            low = chances[2 * pair + side]
            change_c = mm_cols(jnp.where(mine, outer, jnp.zeros_like(outer)), values)
            weight = low.astype(WIDE)
            product = weight * change_c
            scores = (product - weight * jnp.sum(product, axis=-1, keepdims=True)).astype(LOW)
            parts.append((mm(scores, keys), mm_rows(scores, queries), mm_rows(low, outer)))
        for i, scale in ((0, SCALE), (1, SCALE), (2, 1.0)):
            cols = slice(i * HALF + at, i * HALF + at + PAIR)
            value = (jnp.where(first, parts[0][i], parts[1][i]) * scale).astype(LOW)
            change[:, cols] = value
            if i != 1:
                total = jnp.sum(value.astype(WIDE), axis=0, keepdims=True)
                row = i // 2
                sums[row : row + 1, at : at + PAIR] = total * once
                sums[row : row + 1, HALF + at : HALF + at + PAIR] = total * (1.0 - once)
    for i in range(2):
        rows = slice(i * HALF, (i + 1) * HALF)
        part[:, rows] = mm_cols(change[...], w_qkv[rows, : 3 * HALF]).astype(LOW)

def attend_back(place, before, own, got, normed, spread, vec, w_qkv, w_out, mixing, chances, after=()):
    return kernel_call(attend_back_body,
        [((SEQ, D), LOW)] + BACK_OUTS + [((SEQ, 3 * HALF), LOW), ((SEQ, D), LOW), ((8, D), WIDE)],
        (place, before, own, got, normed, spread, vec, w_qkv, w_out, mixing, chances),
        [pltpu.VMEM((SEQ, HALF), LOW)], after)


def source_rows(place, bits, rows):
    starts = []
    for relative in range(1 << len(bits)):
        dp_mask = x_mask = 0
        for i, bit in enumerate(bits):
            if (relative >> (len(bits) - 1 - i)) & 1:
                if bit == "x":
                    x_mask = 1
                else:
                    dp_mask |= 1 << bit
        start = place[1] ^ dp_mask
        if "x" in bits:
            start = start * 2 + (place[2] ^ x_mask)
        start = start * rows
        starts.append(pl.multiple_of(start, 16))
    return starts


def spread_rows(place, bits, whole, kept, sent):
    rows = whole.shape[0] >> len(bits)
    half = 1 << (len(bits) - 1)
    for i, start in enumerate(source_rows(place, bits, rows)):
        target = kept if i < half else sent
        at = (i % half) * rows
        target[at : at + rows, :] = whole[pl.ds(start, rows), :]


def feed_weights_grad(place, active, branch, hidden, change, bits_down, bits_up):
    if (D >> len(bits_down)) % 16:
        plain = lambda a, b: mm_rows(a, b).astype(LOW)
        return plain(active, branch), plain(hidden, change)

    def body(place, active, branch, hidden, change, down_kept, down_sent, up_kept, up_sent, down, up):
        for i in range(WIDTH // HALF):
            rows = slice(i * HALF, (i + 1) * HALF)
            down[rows, :] = mm_rows(active[:, rows], branch[...]).astype(LOW)
        spread_rows(place, bits_down, down, down_kept, down_sent)
        for i in range(WIDTH // HALF):
            cols = slice(i * HALF, (i + 1) * HALF)
            up[:, cols] = mm_rows(hidden[...], change[:, cols]).astype(LOW)
        spread_rows(place, bits_up, up, up_kept, up_sent)

    down = kernel_call(
        body,
        [((WIDTH // 2, D), LOW)] * 2 + [((D // 2, WIDTH), LOW)] * 2,
        (place, active, branch, hidden, change),
        [pltpu.VMEM((WIDTH, D), LOW), pltpu.VMEM((D, WIDTH), LOW)],
    )
    return down[:2], down[2:]


def out_weight_grad(place, count, context, branch):
    rows = D // count
    if (rows // 2) % 16:
        parts = mm_rows(context, branch).astype(LOW).reshape(count // 2, 2, rows // 2, 2, HALF)
        parts = parts.transpose(1, 0, 3, 2, 4).reshape(2, count // 2, rows, HALF)
        first = place[0] == 0
        return jnp.where(first, parts[0], parts[1]), jnp.where(first, parts[1], parts[0])

    def body(place, context, branch, own, other, whole):
        half = rows // 2
        whole[...] = mm_rows(context[...], branch[...]).astype(LOW)
        for j in range(count // 2):
            for target, core in ((own, place[0]), (other, 1 - place[0])):
                start = pl.multiple_of(j * rows + core * half, 16)
                target[j, :half, :] = whole[pl.ds(start, half), :HALF]
                target[j, half:, :] = whole[pl.ds(start, half), HALF:]

    return kernel_call(
        body,
        [((count // 2, rows, HALF), LOW)] * 2,
        (place, context, branch),
        [pltpu.VMEM((HALF, D), LOW)],
    )


def out_weight(place, count, own, got):
    rows = D // count
    half = rows // 2
    if half % 16:
        first = place[0] == 0
        own, got = [p.reshape(count // 2, 2, half, HALF) for p in (own, got)]
        both = jnp.stack([jnp.where(first, own, got), jnp.where(first, got, own)], axis=1)
        return both.transpose(0, 1, 3, 2, 4).reshape(HALF, D)

    def body(place, own, got, whole):
        for i in range(count // 2):
            j = ((((place[1] >> 1) & 1) ^ (i >> 1)) << 1) | (i & 1)
            for source, core in ((own, place[0]), (got, 1 - place[0])):
                start = pl.multiple_of(j * rows + core * half, 16)
                whole[pl.ds(start, half), :HALF] = source[i, :half, :]
                whole[pl.ds(start, half), HALF:] = source[i, half:, :]

    return kernel_call(body, [((HALF, D), LOW)], (place, own, got))[0]


def attend_weights_grad(place, count, hidden, change, out_own, out_got, bits, sums=None):
    rows = D // count
    extra = 0 if sums is None else 16

    def vec_rows(sums):
        attend, feed = [
            jnp.concatenate([part[...][:8] for part in pair], axis=0) for pair in (sums[::2], sums[1::2])
        ]
        row = lax.broadcasted_iota(jnp.int32, (16, 1), 0) % 8
        down = jnp.concatenate(
            [jnp.broadcast_to(part[...][6:7], (8, D)) for part in sums[1::2]], axis=0
        )
        return jnp.concatenate([jnp.where(row == 3, down, attend), feed], axis=1).astype(LOW)

    if (rows // 2) % 16:
        first = place[0] == 0
        out_parts = jnp.concatenate(
            [jnp.where(first, out_own, out_got), jnp.where(first, out_got, out_own)]
        )
        parts = mm_rows(hidden, change).astype(LOW).reshape(count, rows, 3 * HALF)
        whole = jnp.concatenate([parts, out_parts], axis=2).reshape(D, WIDTH)
        return whole if sums is None else (whole, vec_rows(sums))

    def body(place, hidden, change, out_own, out_got, *rest):
        *sums, kept, sent, whole = rest
        for i in range(3):
            cols = slice(i * HALF, (i + 1) * HALF)
            whole[:, cols] = mm_rows(hidden[...], change[:, cols]).astype(LOW)
        for source, core in ((out_own, place[0]), (out_got, 1 - place[0])):
            for j in range(count // 2):
                start = pl.multiple_of((core * (count // 2) + j) * rows, 16)
                whole[pl.ds(start, rows), 3 * HALF :] = source[j]
        spread_rows(place, bits, whole, kept, sent)
        if sums:
            sent[D // 2 :, :] = vec_rows(sums)

    return kernel_call(
        body,
        [((D // 2, WIDTH), LOW), ((D // 2 + extra, WIDTH), LOW)],
        (place, hidden, change, out_own, out_got) + tuple(sums or ()),
        [pltpu.VMEM((D, WIDTH), LOW)],
    )


class Links:
    def __init__(self):
        self.count = lax.axis_size("dp")
        self.bits = self.count.bit_length() - 1
        self.dp = lax.axis_index("dp")
        self.x = lax.axis_index("x")
        self.c = lax.axis_index("c")
        self.plain = (D // self.count // 2) % 16 != 0

    def own(self, bit):
        if bit == "c":
            return self.c
        if bit == "x":
            return self.x
        return (self.dp >> bit) & 1

    def flip(self, value, bit):
        step = {"c": 1, "x": 2}.get(bit)
        if step is None:
            step = 4 << bit
        pairs = [(place, place ^ step) for place in range(4 * self.count)]
        return lax.ppermute(value, AXES, pairs)

    def order(self, names):
        bits = {"x": ["x"], "y": [0], "1": [1], "2": list(range(self.bits))[:1:-1]}
        return [bit for name in names for bit in bits[name]]

class Gather:
    def __init__(self, links, shard, names):
        self.links, self.shape = links, shard.shape
        self.bits = links.order(names)
        self.held = shard.reshape((1,) * len(self.bits) + shard.shape)
        self.got = None
        self.layers = [None, None]

    def axis(self, bit):
        return 0 if bit == "x" else self.links.bits - bit

    def joined(self, held, got, bit):
        first = self.links.own(bit) == 0
        return jnp.concatenate(
            [jnp.where(first, held, got), jnp.where(first, got, held)], axis=self.axis(bit)
        )

    def send(self):
        bit = self.bits[0]
        if len(self.bits) > 1 or bit == "x":
            self.got = self.links.flip(self.held, bit)
        else:
            first = self.links.flip(self.held[:1], bit)
            self.got = [first, self.links.flip(tie(self.held[1:], first), bit)]

    def join(self):
        held = self.held
        self.held = self.joined(held, self.got, self.bits[0])
        self.bits = self.bits[1:]

    def whole(self, layer):
        if self.bits[0] == "x":
            whole = jnp.where(self.links.x == layer, self.held, self.got)
        else:
            whole = self.joined(self.held[layer : layer + 1], self.got[layer], self.bits[0])
        return whole.reshape((self.links.count,) + self.shape)

    def pieces(self, layer):
        if self.bits[0] == "x":
            return [part.reshape((-1,) + self.shape) for part in (self.held, self.got)]
        return [
            part.reshape((-1,) + self.shape) for part in (self.held[layer : layer + 1], self.got[layer])
        ]

    def weight(self, layer, rows, lanes):
        if self.links.plain:
            return self.whole(layer).reshape(rows, lanes)
        bit, size = self.bits[0], self.shape[0]

        def copies(place, refs):
            if bit == "x":
                own = place[2] == layer
                for source, condition in zip(refs, (own, jnp.logical_not(own))):
                    for chip in range(source.shape[0]):
                        yield source.at[chip], chip * size, condition
            else:
                for side, source in enumerate(refs):
                    one = ((place[1] >> bit) & 1) ^ side
                    for i in range(source.shape[0]):
                        chip = ((i >> bit) << (bit + 1)) | (one << bit) | (i & ((1 << bit) - 1))
                        yield source.at[i], chip * size, None

        return Weight((rows, lanes), self.pieces(layer), copies)


class Spread:
    def __init__(self, links, value, names):
        self.links, self.held = links, value
        self.bits = links.order(names)

    def send(self):
        self.got = self.links.flip(self.held, self.bits[0])

    def join(self):
        held, got = self.held, self.got
        if self.bits[0] == "x":
            first = self.links.x == 0
            self.held = jnp.concatenate([jnp.where(first, held, got), jnp.where(first, got, held)])
        else:
            self.held = (held.astype(WIDE) + got.astype(WIDE)).astype(LOW)
        self.bits = self.bits[1:]


class Scatter:
    def __init__(self, links, parts, names, extra=None, pieces=()):
        self.links, self.bits = links, links.order(names)
        self.pieces = list(pieces) + [1] * len(self.bits)
        self.plain = links.plain
        self.extra = extra
        if self.plain:
            self.kept = parts
        else:
            self.kept, self.sent = parts
            if extra is not None:
                self.extra = self.sent[self.kept.shape[0] :]

    def send(self):
        if not self.plain:
            number = self.pieces.pop(0)
            size = self.kept.shape[0] // number
            cuts = [i * size for i in range(number)] + [self.sent.shape[0]]
            self.got = tuple(
                self.links.flip(self.sent[a:b], self.bits[0]) for a, b in zip(cuts, cuts[1:])
            )

    def add(self, token, after=()):
        if self.plain:
            if self.bits:
                self.add_plain(tie(self.kept, token))
            return self.kept
        kept = tie(self.kept, token)
        self.kept, self.sent, self.extra = add_rows(kept, self.got, self.extra, len(self.bits) == 1, after)
        self.bits = self.bits[1:]
        return self.kept

    def add_plain(self, parts):
        links, lanes = self.links, parts.shape[1]
        has_x = "x" in self.bits
        held = parts.reshape((2,) * (links.bits + has_x) + (-1, lanes))
        for bit in self.bits:
            own, axis = links.own(bit), links.bits if bit == "x" else links.bits - 1 - bit
            kept = lax.dynamic_slice_in_dim(held, own, 1, axis)
            sent = lax.dynamic_slice_in_dim(held, 1 - own, 1, axis)
            if self.extra is None:
                got = links.flip(sent, bit)
            else:
                got = links.flip(jnp.concatenate([sent.reshape(-1, lanes), self.extra]), bit)
                split = got.shape[0] - self.extra.shape[0]
                self.extra = (self.extra.astype(WIDE) + got[split:].astype(WIDE)).astype(LOW)
                got = got[:split].reshape(sent.shape)
            held = (kept.astype(WIDE) + got.astype(WIDE)).astype(LOW)
        self.kept, self.bits = held.reshape(-1, lanes), []


class Pair:
    def __init__(self, w, u):
        self.w, self.u = w, u

    def merge(self, token, after=()):
        w, u = self.w, self.u
        if w.plain:
            half = u.add(w.add(token)).shape[0]
            self.kept = jnp.concatenate(
                [u.kept, jnp.concatenate([w.kept[:half], w.kept[half:]], axis=1)]
            )
            return self.kept
        half = u.kept.shape[0] // 2

        def body(place, w_kept, w_got, u_kept, u_got, kept, sent):
            for at, target in ((0, kept), (half, sent)):
                rows = slice(at, at + half)
                target[:half, :] = (
                    u_kept[rows, :].astype(WIDE) + u_got[rows, :].astype(WIDE)
                ).astype(LOW)
                for i in range(2):
                    rows = slice(2 * at + i * half, 2 * at + (i + 1) * half)
                    target[half:, i * D : (i + 1) * D] = (
                        w_kept[rows, :].astype(WIDE) + w_got[rows, :].astype(WIDE)
                    ).astype(LOW)

        self.kept, sent = kernel_call(
            body,
            [((2 * half, WIDTH), LOW)] * 2,
            (jnp.zeros((1,), jnp.int32), tie(w.kept, token), w.got[0], u.kept, u.got[0]),
            after=after,
        )
        self.got = w.links.flip(sent, w.bits[1])
        return self.kept

    def finish(self, token, after=()):
        if self.w.plain:
            return self.kept

        def body(place, kept, got, out):
            out[...] = (kept[...].astype(WIDE) + got[...].astype(WIDE)).astype(LOW)

        self.kept = kernel_call(
            body,
            [(self.kept.shape, LOW)],
            (jnp.zeros((1,), jnp.int32), tie(self.kept, token), self.got),
            after=after,
        )[0]
        return self.kept


def tie(value, token):
    return lax.optimization_barrier((value, token))[0]


def add_rows(kept, got, extra, last, after):
    rows, lanes = kept.shape
    more = 0 if extra is None else extra.shape[0]
    half = rows if last else rows // 2

    def body(place, kept, got, *rest):
        size = rows // len(got)
        if more:
            extra_sum = (rest[0][...].astype(WIDE) + got[-1][size:, :].astype(WIDE)).astype(LOW)
            rest[-1][...] = extra_sum
            rest = rest[1:-1]
            if not last:
                rest[1][half:, :] = extra_sum
        step = min(size, half)
        for at in range(0, rows, step):
            piece = got[at // size]
            start = at % size
            total = (
                kept[at : at + step, :].astype(WIDE) + piece[start : start + step, :].astype(WIDE)
            ).astype(LOW)
            target, to = (rest[0], at) if at < half else (rest[1], at - half)
            target[to : to + step, :] = total

    outs = [((half, lanes), LOW)]
    if not last:
        outs.append(((half + more, lanes), LOW))
    if more:
        outs.append(((more, lanes), LOW))
    ins = (jnp.zeros((1,), jnp.int32), kept, got) + ((extra,) if more else ())
    results = list(kernel_call(body, outs, ins, after=after))
    extra = results.pop() if more else None
    return results[0], None if last else results[1], extra


def adam_update(master, first, second, gradient):
    first_new = BETA_ONE * first + (1.0 - BETA_ONE) * gradient
    second_new = BETA_TWO * second + (1.0 - BETA_TWO) * gradient * gradient
    update = first_new / BIAS_ONE / (jnp.sqrt(second_new / BIAS_TWO) + ADAM_EPSILON)
    return (update + WEIGHT_DECAY * master, first_new, second_new)


def on_device(
    inputs,
    cotangent,
    in_master,
    in_first,
    in_second,
    down_master,
    down_first,
    down_second,
    vec_master,
    vec_first,
    vec_second,
):
    links = Links()
    count, x, c = links.count, links.x, links.c
    rows = D // count
    half_rows = rows // 2
    vec_part = VEC // count
    first_core = c == 0
    first_chip = x == 0
    place = jnp.stack([c, links.dp, x]).astype(jnp.int32)

    def mine(one, other):
        return jnp.where(first_core, one, other)

    def trade(part):
        return links.flip(part, "c")

    def trade_blocks(part):
        return tuple(trade(part[i : i + BLOCK]) for i in range(0, SEQ, BLOCK))

    in_low = in_master[0].astype(LOW)
    out_rows = in_low[:, 3 * D :]
    pieces = []
    for core in (0, 1):
        out_half = out_rows[core * half_rows : (core + 1) * half_rows]
        pieces.append(
            jnp.concatenate(
                [in_low[:, i * D + core * HALF : i * D + (core + 1) * HALF] for i in range(3)]
                + [jnp.concatenate([out_half[:, :HALF], out_half[:, HALF:]], axis=0)],
                axis=1,
            )
        )
    got = trade(mine(pieces[1], in_low[:, :WIDTH]))
    attend_shard = mine(pieces[0], got)
    up_shard = mine(got, in_low[:, WIDTH:])
    down_shard = down_master[0].astype(LOW)

    placed = lax.dynamic_update_slice(
        jnp.zeros((VEC,), WIDE), vec_master[0], (links.dp * vec_part,)
    ).reshape(-1, D)
    high = lax.reduce_precision(placed, 8, 7)
    vec_both = jnp.pad(jnp.concatenate([high, placed - high]).astype(LOW), ((0, 4), (0, 0)))
    vec_got = trade(vec_both)
    vec_both = jnp.concatenate([mine(vec_both, vec_got), mine(vec_got, vec_both)])

    small = Spread(links, vec_both, "yx21")
    attend_in = Gather(links, attend_shard, "2xy1")
    down_in = Gather(links, down_shard, "2y1x")
    up_in = Gather(links, up_shard, "12xy")
    streams = {"v": small, "t": attend_in, "w": down_in, "u": up_in}
    for name in "twu":
        streams[name].send()
    small.held = tie(small.held, attend_in.got)
    small.send()
    turns = "tvwuvtwuvtwvu" if links.bits == 3 else "twuv" * links.bits + "v"
    for name in turns:
        streams[name].join()
        if streams[name].bits:
            streams[name].send()
    vectors = small.held.reshape(2, 32, D)
    vecs = []
    for layer in (0, 1):
        vec = vectors[layer].astype(WIDE)
        vecs.append([vec[i : i + 6] + vec[i + 6 : i + 12] for i in (0, 16)])

    def attend_weights(layer):
        if links.plain:
            parts = attend_in.whole(layer)[None]
        else:
            parts = jnp.stack(attend_in.pieces(layer))
        parts = parts[..., 3 * HALF :].reshape(parts.shape[0], 2, -1, rows, HALF)
        own = mine(parts[:, 0], parts[:, 1]).reshape(-1, rows, HALF)
        got = trade(mine(parts[:, 1], parts[:, 0]).reshape(-1, rows, HALF))
        return attend_in.weight(layer, D, WIDTH), out_weight(place, count, own, got)

    qkv, out, up, down = [None] * 2, [None] * 2, [None] * 2, [None] * 2
    qkv[0], out[0] = attend_weights(0)
    hidden = [lax.dynamic_slice_in_dim(inputs, x * SEQ, SEQ, 0)]
    part, mixing_0, chances_0, context_0 = attend_first(
        place, hidden[0], qkv[0], out[0], vecs[0][0]
    )
    up[0] = up_in.weight(0, D, WIDTH)
    down[0] = down_in.weight(0, WIDTH, D)
    next_hidden, normed_0, spread_0, part, active_0, slope_0 = feed_forward(
        place, hidden[0], part, trade_blocks(part), vecs[0][0], vecs[0][1], up[0], down[0]
    )
    hidden.append(next_hidden)
    qkv[1], out[1] = attend_weights(1)
    next_hidden, normed_1, spread_1, part, mixing_1, chances_1, context_1 = attend_next(
        place, hidden[1], part, trade_blocks(part), vecs[0][1], vecs[0][0], qkv[1], out[1], vecs[1][0]
    )
    hidden.append(next_hidden)
    up[1] = up_in.weight(1, D, WIDTH)
    down[1] = down_in.weight(1, WIDTH, D)
    next_hidden, normed_2, spread_2, part, active_1, slope_1 = feed_forward(
        place, hidden[2], part, trade_blocks(part), vecs[1][0], vecs[1][1], up[1], down[1]
    )
    hidden.append(next_hidden)

    class Sections:
        def __init__(self, values):
            low, high = mine(values[0], values[1]), mine(values[2], values[3])
            self.own = jnp.where(first_chip, low, high)
            self.away = jnp.where(first_chip, high, low)

        def send(self, token):
            self.got = links.flip(tie(self.away, token), "x")

        def whole(self):
            return jnp.concatenate(
                [jnp.where(first_chip, self.own, self.got), jnp.where(first_chip, self.got, self.own)]
            )[None]

    def home(one, other):
        got = links.flip(jnp.where(first_chip, other, one), "x")
        own = jnp.where(first_chip, one, other)
        return jnp.where(first_chip, own, got), jnp.where(first_chip, got, own)

    names = {"w": "x12y", "u": "1x2y", "t": "y12", "T": "y12", "W": "xy12", "U": "1xy2"}
    bits = {name: links.order(order) for name, order in names.items()}

    def feed_sums(layer, active, branch, hidden, change):
        both = "wu" if layer else "WU"
        parts = feed_weights_grad(
            place, active, branch, hidden, change, bits[both[0]], bits[both[1]]
        )
        sums = [Scatter(links, part, names[name]) for part, name in zip(parts, both)]
        for each in sums:
            each.send()
        return sums

    def attend_sums(layer, context, branch, hidden, change, vector_sums=None):
        own = "t" if vector_sums is None else "T"
        out_own, out_other = out_weight_grad(place, count, context, branch)
        parts = attend_weights_grad(
            place, count, hidden, change, out_own, trade(out_other), bits[own], vector_sums
        )
        extra = None
        if vector_sums is not None:
            parts, extra = parts if links.plain else (parts, True)
        total = Scatter(links, parts, names[own], extra)
        total.send()
        return total

    cotangent_rows = lax.dynamic_slice_in_dim(cotangent, x * SEQ, SEQ, 0)
    last, summed, branch, change, part, feed_vec_1 = feed_last(
        place, hidden[3], part, trade_blocks(part), vecs[1][0], vecs[1][1], up[1], down[1], slope_1, cotangent_rows
    )
    part_got = trade_blocks(part)
    outputs = Sections(hidden[1:] + [last])
    w_1, u_1 = feed_sums(1, active_1, branch, hidden[3], change)
    grad_3, summed, branch, change, part, attend_vec_1 = attend_back(
        place, tie(summed, u_1.kept), part, part_got, normed_2, spread_2, vecs[1][0], qkv[1], out[1], mixing_1, chances_1
    )
    part_got = trade_blocks(part)
    t_1 = attend_sums(1, context_1, branch, hidden[2], change)
    grad_2, summed, branch, change, part, feed_vec_0 = feed_back(
        place, tie(summed, t_1.kept), part, part_got, normed_1, spread_1, vecs[0][1], up[0], down[0], slope_0
    )
    part_got = trade_blocks(part)
    token = w_1.add(branch)
    w_1.send()
    token = u_1.add(token)
    u_1.send()
    w_0, u_0 = feed_sums(0, active_0, tie(branch, token), hidden[1], change)
    outputs.send(t_1.kept)
    token = u_0.kept
    grad_1, summed, branch, change, part, attend_vec_0 = attend_back(
        place, tie(summed, token), part, part_got, normed_0, spread_0, vecs[0][0], qkv[0], out[0], mixing_0, chances_0, (outputs.got,)
    )
    part_got = trade_blocks(part)
    token = t_1.add(grad_1)
    t_1.send()
    token = w_1.add(token)
    w_1.send()
    token = u_1.add(token)
    u_1.send()
    t_0 = attend_sums(
        0,
        context_0,
        tie(branch, token),
        hidden[0],
        change,
        (attend_vec_0, feed_vec_0, attend_vec_1, feed_vec_1),
    )
    grad_0 = (summed + part.astype(WIDE) + jnp.concatenate(part_got).astype(WIDE)).astype(LOW)
    grads = Sections([grad_0, grad_1, grad_2, grad_3])
    token = t_0.kept
    sums = {"w": w_1, "u": u_1, "t": t_1, "W": w_0, "U": u_0, "T": t_0}
    pairs = {"p": Pair(w_1, u_1), "P": Pair(w_0, u_0)}
    pairs["q"], pairs["Q"] = pairs["p"], pairs["P"]
    after = ()
    for name in ORDER:
        if name == "o":
            outputs.send(token)
        elif name == "g":
            grads.send(token)
        elif name in "OG":
            after = (outputs.got,) if name == "O" else (grads.got,)
        elif name in "pP":
            token, after = pairs[name].merge(token, after), ()
        elif name in "qQ":
            token, after = pairs[name].finish(token, after), ()
        else:
            token = sums[name].add(token, after)
            after = ()
            if sums[name].bits:
                sums[name].send()
            elif name == "T":
                sent = jnp.concatenate([jnp.where(first_chip, t_1.kept, t_0.kept), t_0.extra])
                last_got = links.flip(sent, "x")
    ours, other = home(pairs["P"].kept, pairs["p"].kept)
    up_sum = jnp.concatenate([ours[:half_rows], other[:half_rows]])
    down_sum = jnp.concatenate(
        [part[half_rows:, at : at + D] for part in (ours, other) for at in (0, D)]
    )

    got = last_got
    attend_sum = jnp.where(first_chip, t_0.kept, t_1.kept).astype(WIDE) + got[:rows].astype(WIDE)
    attend_sum = attend_sum.astype(LOW)
    vec_total = (t_0.extra.astype(WIDE) + got[rows:].astype(WIDE)).astype(LOW)
    section_outputs, section_input_grads = outputs.whole(), grads.whole()

    got = trade(jnp.concatenate([mine(up_sum, attend_sum), vec_total]))
    vec_total = vec_total.astype(WIDE) + got[rows:].astype(WIDE)
    got = got[:rows]
    kept = mine(attend_sum, up_sum)
    first, second = mine(kept, got), mine(got, kept)

    def joined(one, other):
        out_one, out_other = one[:, 3 * HALF :], other[:, 3 * HALF :]
        out_cols = [
            jnp.concatenate([out_one[i : i + half_rows], out_other[i : i + half_rows]])
            for i in (0, half_rows)
        ]
        cols = [part[:, i * HALF : (i + 1) * HALF] for i in range(3) for part in (one, other)]
        return jnp.concatenate(cols + out_cols, axis=1)

    in_sum = mine(joined(first, second), jnp.concatenate([first, second], axis=1))
    in_sum = in_sum.astype(WIDE)[None]
    down_sum = down_sum.astype(WIDE)[None]
    vec_sum = lax.dynamic_slice(vec_total, (8 * x, D * c), (6, D)).reshape(VEC)
    vec_sum = lax.dynamic_slice(vec_sum, (links.dp * vec_part,), (vec_part,))[None]

    in_step, in_first_new, in_second_new = adam_update(in_master, in_first, in_second, in_sum)
    down_step, down_first_new, down_second_new = adam_update(
        down_master, down_first, down_second, down_sum
    )
    vec_step, vec_first_new, vec_second_new = adam_update(
        vec_master, vec_first, vec_second, vec_sum
    )
    return (
        section_outputs,
        section_input_grads,
        in_sum,
        down_sum,
        vec_sum,
        in_step,
        in_first_new,
        in_second_new,
        down_step,
        down_first_new,
        down_second_new,
        vec_step,
        vec_first_new,
        vec_second_new,
    )


def solution(mesh):
    grid = Mesh(mesh.devices.reshape(mesh.shape["dp"], 2, 2), AXES)
    tokens = P("dp", None)
    matrix = P(("x", "c"), "dp", None)
    vector = P(("x", "c"), "dp")
    return jax.shard_map(
        on_device,
        mesh=grid,
        in_specs=(tokens,) * 2 + (matrix,) * 6 + (vector,) * 3,
        out_specs=(matrix,) * 4 + (vector,) + (matrix,) * 6 + (vector,) * 3,
        check_vma=False,
    )
```
